32 devices in a mesh: blk: 8 (over y, x, core), grp: 4 (over z).
Axes of the slice: x: 2, y: 2, z: 4, core: 2. Of those that a mesh axis runs over, the one named last changes fastest.
Arguments:
- images: bfloat16 [64, 3, 1024], P(('blk', 'grp')), may hold values from -10 to 10
Outputs:
- kernel_window: float32 [64, 5, 8], P(('blk', 'grp'))
The draws below stay inside these ranges and needn't reach their ends.
All inputs are finite; a program needn't handle non-finite values.
Results may differ from the reference program's by a relative error of at most 0.0003.
Values may be sent and summed in bfloat16 or wider, within the bound.
A program may use at most 64 MiB of HBM per device.

```python
import math
import jax
import jax.numpy as jnp
from jax import lax

SIDE = 32
PIX = 1024
CHAN = 3
LAYERS = 3
ROUNDS = 2
BLOCK = 8
IMAGES = 64
SPAN = 5
N_BLK = 8


class_total = 10


def smooth_wave(key, lead_shape):
    subkeys = jax.random.split(key, 4)
    freq_rows = jax.random.uniform(subkeys[0], lead_shape + (1,), minval=0.0, maxval=3.0)
    phase_rows = jax.random.uniform(subkeys[1], lead_shape + (1,), minval=-math.pi, maxval=math.pi)
    freq_cols = jax.random.uniform(subkeys[2], lead_shape + (1,), minval=0.0, maxval=3.0)
    phase_cols = jax.random.uniform(subkeys[3], lead_shape + (1,), minval=-math.pi, maxval=math.pi)
    pixel_index = jnp.arange(PIX)
    row_pos = (pixel_index // SIDE).astype(jnp.float32) / SIDE
    col_pos = (pixel_index % SIDE).astype(jnp.float32) / SIDE
    return jnp.cos(math.pi * freq_rows * row_pos + phase_rows) * jnp.cos(math.pi * freq_cols * col_pos + phase_cols)


def draw_images(key, part):
    key = jax.random.fold_in(key, 11)
    subkeys = jax.random.split(key, 8)
    shared = 0.8 + 0.15 * smooth_wave(subkeys[0], (CHAN,)) + 0.15 * smooth_wave(subkeys[1], (CHAN,))
    class_fields = 0.35 * smooth_wave(subkeys[2], (class_total, CHAN)) + 0.35 * smooth_wave(subkeys[3], (class_total, CHAN))
    labels = jax.random.randint(subkeys[4], (IMAGES,), 0, class_total)
    signal = shared[None, :, :] + jnp.take(class_fields, labels, axis=0)
    noise_level = jnp.exp(jax.random.uniform(subkeys[5], (IMAGES, 1, 1), minval=math.log(0.1), maxval=math.log(2.5)))
    gains = jax.random.uniform(subkeys[6], (IMAGES, 1, 1), minval=0.7, maxval=1.3)
    noise = jnp.clip(jax.random.normal(subkeys[7], (IMAGES, CHAN, PIX)), -3.0, 3.0)
    return (gains * signal + noise_level * noise).astype(jnp.bfloat16)


def setup_inputs(seed: int = 0) -> dict:
    seeds = jax.random.split(jax.random.key(seed), 2)
    return {
        "images": draw_images(jax.random.fold_in(seeds[1], 71), 0),
    }


bias_var = 0.1

def stencil_band(side):
    positions = jnp.arange(side)
    return (jnp.abs(positions[:, None] - positions[None, :]) <= 1).astype(jnp.float32)

def stencil_maps(pair_maps, band_matrix):
    shaped = pair_maps.reshape(pair_maps.shape[:-1] + (SIDE, SIDE))
    first = jnp.einsum('ab,...bc->...ac', band_matrix, shaped, precision=lax.Precision.HIGHEST)
    second = jnp.einsum('...ac,dc->...ad', first, band_matrix, precision=lax.Precision.HIGHEST)
    return (second / 9.0).reshape(pair_maps.shape)

def variance_maps(image_data, band_matrix):
    current = stencil_maps(lax.optimization_barrier(jnp.mean(image_data * image_data, axis=1)), band_matrix) + bias_var
    layers_out = [current]
    for layer in range(LAYERS - 1):
        current = stencil_maps(current, band_matrix) + bias_var
        layers_out.append(current)
    return jnp.stack(layers_out, 0)

def relu_expect(cov_map, var_left, var_right):
    scale_root = jnp.sqrt(var_left * var_right)
    ratio = jnp.clip(cov_map / scale_root, -1.0, 1.0)
    angle_map = jnp.arccos(ratio)
    return scale_root * (jnp.sqrt(1.0 - ratio * ratio) + (jnp.pi - angle_map) * ratio) / (2.0 * jnp.pi)

def pair_kernel(left_img, right_img, left_var, right_var, band_matrix):
    product = jnp.einsum('acp,bcp->abp', left_img, right_img, preferred_element_type=jnp.float32) / left_img.shape[1]
    cov_map = stencil_maps(product, band_matrix) + bias_var
    expect = cov_map
    for layer in range(LAYERS):
        expect = relu_expect(cov_map, left_var[layer][:, None, :], right_var[layer][None, :, :])
        if layer < LAYERS - 1:
            cov_map = 2.0 * stencil_maps(expect, band_matrix) + bias_var
    return lax.optimization_barrier(jnp.mean(2.0 * expect, axis=-1))

def reference(images):
    band_matrix = stencil_band(SIDE)
    image_data = images.astype(jnp.float32)
    all_var = variance_maps(image_data, band_matrix)
    blocked = images.reshape(N_BLK, BLOCK, CHAN, PIX)
    blocked_var = all_var.reshape(LAYERS, N_BLK, BLOCK, PIX)

    def one_block(block_index):
        rows_img = blocked[block_index]
        rows_var = blocked_var[:, block_index]
        kernel_tiles = []
        for offset in range(-ROUNDS, ROUNDS + 1):
            other = ((block_index + offset + N_BLK) % N_BLK).astype(jnp.int32)
            kernel_tiles.append(pair_kernel(rows_img, blocked[other], rows_var, blocked_var[:, other], band_matrix))
        return jnp.stack(kernel_tiles, 1)
    result = lax.map(one_block, jnp.arange(N_BLK).astype(jnp.int32))
    return result.reshape(IMAGES, SPAN, BLOCK)
```

```python
import functools
import math

import jax
import jax.numpy as jnp
from jax import lax
from jax.experimental import pallas as pl
from jax.experimental.pallas import tpu as pltpu
from jax.sharding import PartitionSpec as P

SIDE = 32
LAYERS = 3
ROUNDS = 2
SPAN = 2 * ROUNDS + 1
LANES = 128
ROWS = 8
BIAS = 0.1
MESH = pl.DeviceIdType.MESH

ARC = (
    0.31830988122327397,
    -0.022534660160951844,
    0.005977264482236005,
    -0.0024073736878517066,
    0.0010804572825488274,
    -0.0003963123703673673,
    7.618722193421786e-05,
)


def stencil_sum(maps, masks):
    first, last, not_left, not_right = masks
    chunks = len(maps)
    down = [pltpu.roll(x, SIDE, 1) for x in maps]
    up = [pltpu.roll(x, LANES - SIDE, 1) for x in maps]
    sums = []
    for k in range(chunks):
        above = jnp.where(first, down[k - 1] if k else 0.0, down[k])
        below = jnp.where(last, up[k + 1] if k < chunks - 1 else 0.0, up[k])
        sums.append(maps[k] + above + below)
    out = []
    for x in sums:
        left = jnp.where(not_left, pltpu.roll(x, 1, 1), 0.0)
        right = jnp.where(not_right, pltpu.roll(x, LANES - 1, 1), 0.0)
        out.append(x + left + right)
    return out


def lane_masks():
    lane = lax.broadcasted_iota(jnp.int32, (ROWS, LANES), 1)
    col = lane % SIDE
    return lane < SIDE, lane >= LANES - SIDE, col != 0, col != SIDE - 1


def channel_sum(terms):
    total = terms[0]
    for term in terms[1:]:
        total = total + term
    return total


def variance_roots(squares, channels, masks):
    current = [x * (1.0 / (9 * channels)) + BIAS for x in stencil_sum(squares, masks)]
    layers = []
    for layer in range(LAYERS):
        inverse = [lax.rsqrt(x) for x in current]
        layers.append(([x * y for x, y in zip(current, inverse)], inverse))
        if layer < LAYERS - 1:
            current = [x * (1.0 / 9) + BIAS for x in stencil_sum(current, masks)]
    return layers


def twice_relu(cov, scale, inverse):
    a = jnp.minimum(jnp.abs(cov) * inverse, 1.0)
    y = jnp.maximum(1.0 - a, 1e-30)
    poly = ARC[-1]
    for c in ARC[-2::-1]:
        poly = poly * a + c
    bent = y * y * lax.rsqrt(y) * poly
    return scale * bent + jnp.minimum(jnp.maximum(cov, 0.0), scale)


def kernel(
    n_blk, n_grp, images, out, got, own, flat, root, inv, wide, res,
    grp_send, grp_recv, blk_send, blk_recv,
):
    b, z = lax.axis_index("blk"), lax.axis_index("grp")
    chan, per, pix = images.shape
    chunks = pix // LANES
    image_rows = chan * chunks
    block = per * n_grp
    units = block // ROWS
    sources = ROWS // per
    offsets = [d for d in range(-ROUNDS, ROUNDS + 1) if d]

    barrier = pltpu.get_barrier_semaphore()
    for dz in range(1, n_grp):
        pl.semaphore_signal(
            barrier, inc=1, device_id={"grp": lax.rem(z + dz, n_grp)}, device_id_type=MESH
        )
    for d in offsets:
        pl.semaphore_signal(
            barrier, inc=1, device_id={"blk": lax.rem(b + d + n_blk, n_blk)}, device_id_type=MESH
        )

    data = images[...].astype(jnp.float32)
    for i in range(per):
        for k in range(chunks):
            flat[pl.ds(i * image_rows + k, chan, stride=chunks), :] = data[
                :, i, k * LANES : (k + 1) * LANES
            ]
    got[ROUNDS, z] = flat[...].astype(jnp.bfloat16)

    pl.semaphore_wait(barrier, n_grp - 1 + len(offsets))

    copies = []
    for dz in range(1, n_grp):
        copy = pltpu.make_async_remote_copy(
            src_ref=got.at[ROUNDS, z],
            dst_ref=got.at[ROUNDS, z],
            send_sem=grp_send.at[dz],
            recv_sem=grp_recv.at[z],
            device_id={"grp": lax.rem(z + dz, n_grp)},
            device_id_type=MESH,
        )
        copy.start()
        copies.append(copy)

    def pass_on(source, order):
        for at, d in enumerate(offsets):
            copy = pltpu.make_async_remote_copy(
                src_ref=got.at[ROUNDS, source],
                dst_ref=got.at[ROUNDS + d, source],
                send_sem=blk_send.at[order, at],
                recv_sem=blk_recv.at[ROUNDS + d, source],
                device_id={"blk": lax.rem(b - d + n_blk, n_blk)},
                device_id_type=MESH,
            )
            copy.start()
            copies.append(copy)

    pass_on(z, 0)

    masks = lane_masks()
    for i in range(per):
        squares = []
        for k in range(chunks):
            parts = []
            for c in range(chan):
                row = i * image_rows + c * chunks + k
                part = jnp.broadcast_to(flat[row : row + 1, :], (ROWS, LANES))
                own[row] = part
                parts.append(part * part)
            squares.append(channel_sum(parts))
        for layer, (roots, inverses) in enumerate(variance_roots(squares, chan, masks)):
            for k in range(chunks):
                at = (i * LAYERS + layer) * chunks + k
                root[at] = roots[k]
                inv[at] = inverses[k]

    def arrived(k, source, sem):
        pltpu.make_async_remote_copy(
            src_ref=got.at[k, source],
            dst_ref=got.at[k, source],
            send_sem=grp_send.at[0],
            recv_sem=sem,
            device_id={"grp": z},
            device_id_type=MESH,
        ).wait_recv()

    for dz in range(1, n_grp):
        source = lax.rem(z + dz, n_grp)
        arrived(ROUNDS, source, grp_recv.at[source])
        pass_on(source, dz)

    def one_unit(k, unit):
        for s in range(sources):
            wide[s * per * image_rows : (s + 1) * per * image_rows, :] = got[
                k, unit * sources + s
            ].astype(jnp.float32)
        theirs = [
            [wide[pl.ds(c * chunks + j, ROWS, stride=image_rows), :] for c in range(chan)]
            for j in range(chunks)
        ]
        layers = variance_roots(
            [channel_sum([x * x for x in parts]) for parts in theirs], chan, masks
        )
        for i in range(per):
            cov = [
                channel_sum(
                    [own[i * image_rows + c * chunks + j] * theirs[j][c] for c in range(chan)]
                )
                for j in range(chunks)
            ]
            factor = 1.0 / (9 * chan)
            for layer in range(LAYERS):
                at = (i * LAYERS + layer) * chunks
                roots, inverses = layers[layer]
                cov = [x * factor + BIAS for x in stencil_sum(cov, masks)]
                cov = [
                    twice_relu(cov[j], root[at + j] * roots[j], inv[at + j] * inverses[j])
                    for j in range(chunks)
                ]
                factor = 1.0 / 9
            at = ((i * SPAN + k) * units + unit) * ROWS
            res[pl.ds(pl.multiple_of(at, ROWS), ROWS), :] = channel_sum(cov)

    def one_block(t, carry):
        half = (t + 1) // 2
        k = ROUNDS + half * (1 - 2 * (t % 2))

        @pl.when(t > 0)
        def _():
            for source in range(n_grp):
                arrived(k, source, blk_recv.at[k, source])

        for unit in range(units):
            one_unit(k, unit)
        return carry

    lax.fori_loop(0, SPAN, one_block, 0)

    sums = lax.dot_general(
        jnp.full((ROWS, LANES), 1.0 / pix, jnp.float32),
        res[...],
        (((1,), (1,)), ((), ())),
        precision=lax.Precision.HIGHEST,
        preferred_element_type=jnp.float32,
    )
    out[...] = sums[0:1, :]
    for copy in copies:
        copy.wait_send()


def per_device(n_blk, n_grp, images):
    per, chan, pix = images.shape
    chunks = pix // LANES
    rows = per * chan * chunks
    block = per * n_grp
    assert block % ROWS == 0 and ROWS % per == 0
    total = per * SPAN * block
    maps = per * LAYERS * chunks
    sums = pl.pallas_call(
        functools.partial(kernel, n_blk, n_grp),
        out_shape=jax.ShapeDtypeStruct((1, total), jnp.float32),
        in_specs=[pl.BlockSpec(memory_space=pltpu.VMEM)],
        out_specs=pl.BlockSpec(memory_space=pltpu.VMEM),
        scratch_shapes=[
            pltpu.VMEM((SPAN, n_grp, rows, LANES), jnp.bfloat16),
            pltpu.VMEM((rows, ROWS, LANES), jnp.float32),
            pltpu.VMEM((rows, LANES), jnp.float32),
            pltpu.VMEM((maps, ROWS, LANES), jnp.float32),
            pltpu.VMEM((maps, ROWS, LANES), jnp.float32),
            pltpu.VMEM((ROWS * chan * chunks, LANES), jnp.float32),
            pltpu.VMEM((total, LANES), jnp.float32),
            pltpu.SemaphoreType.DMA((n_grp,)),
            pltpu.SemaphoreType.DMA((n_grp,)),
            pltpu.SemaphoreType.DMA((n_grp, SPAN - 1)),
            pltpu.SemaphoreType.DMA((SPAN, n_grp)),
        ],
        compiler_params=pltpu.CompilerParams(
            collective_id=0, has_side_effects=True, vmem_limit_bytes=16 * 1024 * 1024
        ),
    )(jnp.transpose(images, (1, 0, 2)))
    return sums.reshape(per, SPAN, block)


def solution(mesh):
    spec = P(("blk", "grp"), None, None)
    body = functools.partial(per_device, mesh.shape["blk"], mesh.shape["grp"])
    return jax.shard_map(body, mesh=mesh, in_specs=(spec,), out_specs=spec, check_vma=False)
```

```python
import functools

import jax
import jax.numpy as jnp
from jax import lax
from jax.experimental import pallas as pl
from jax.experimental.pallas import tpu as pltpu
from jax.sharding import PartitionSpec as P

SIDE = 32
LAYERS = 3
ROUNDS = 2
SPAN = 2 * ROUNDS + 1
LANES = 128
ROWS = 8
BIAS = 0.1
BELOW_ONE = 1.0 - 2.0**-24
MESH = pl.DeviceIdType.MESH

ARC = (
    0.3183098449892848,
    -0.02253203775558662,
    0.005946535585369838,
    -0.002275705294168609,
    0.0008254564785290766,
    -0.00016869743862866002,
)


def stencil_sum(maps, masks):
    first, last, not_left, not_right = masks
    chunks = len(maps)
    down = [pltpu.roll(x, SIDE, 1) for x in maps]
    up = [pltpu.roll(x, LANES - SIDE, 1) for x in maps]
    sums = []
    for k in range(chunks):
        above = jnp.where(first, down[k - 1] if k else 0.0, down[k])
        below = jnp.where(last, up[k + 1] if k < chunks - 1 else 0.0, up[k])
        sums.append(maps[k] + above + below)
    out = []
    for x in sums:
        left = jnp.where(not_left, pltpu.roll(x, 1, 1), 0.0)
        right = jnp.where(not_right, pltpu.roll(x, LANES - 1, 1), 0.0)
        out.append(x + left + right)
    return out


def lane_masks():
    lane = lax.broadcasted_iota(jnp.int32, (ROWS, LANES), 1)
    col = lane % SIDE
    return lane < SIDE, lane >= LANES - SIDE, col != 0, col != SIDE - 1


def channel_sum(terms):
    total = terms[0]
    for term in terms[1:]:
        total = total + term
    return total


def variance_roots(squares, channels, masks):
    current = [x * (1.0 / (9 * channels)) + BIAS for x in stencil_sum(squares, masks)]
    layers = []
    for layer in range(LAYERS):
        inverse = [lax.rsqrt(x) for x in current]
        layers.append(([x * y for x, y in zip(current, inverse)], inverse))
        if layer < LAYERS - 1:
            current = [x * (1.0 / 9) + BIAS for x in stencil_sum(current, masks)]
    return layers


def twice_relu(cov, scale, inverse):
    a = jnp.minimum(jnp.abs(cov) * inverse, BELOW_ONE)
    y = 1.0 - a
    poly = ARC[-1]
    for c in ARC[-2::-1]:
        poly = poly * a + c
    bent = y * y * lax.rsqrt(y) * poly
    return scale * bent + jnp.minimum(jnp.maximum(cov, 0.0), scale)


def kernel(
    n_blk, n_grp, images, out, raw, got, own, flat, root, inv, wide, res,
    raw_sem, grp_send, grp_recv, blk_send, blk_recv,
):
    b, z = lax.axis_index("blk"), lax.axis_index("grp")
    chan, per, pix = images.shape
    chunks = pix // LANES
    image_rows = chan * chunks
    block = per * n_grp
    units = block // ROWS
    sources = ROWS // per
    offsets = [d for d in range(-ROUNDS, ROUNDS + 1) if d]

    load = pltpu.make_async_copy(images, raw, raw_sem)
    load.start()
    barrier = pltpu.get_barrier_semaphore()
    for dz in range(1, n_grp):
        pl.semaphore_signal(
            barrier, inc=1, device_id={"grp": lax.rem(z + dz, n_grp)}, device_id_type=MESH
        )
    for d in offsets:
        pl.semaphore_signal(
            barrier, inc=1, device_id={"blk": lax.rem(b + d + n_blk, n_blk)}, device_id_type=MESH
        )
    load.wait()

    data = raw[...].astype(jnp.float32)
    for i in range(per):
        for k in range(chunks):
            flat[pl.ds(i * image_rows + k, chan, stride=chunks), :] = data[
                :, i, k * LANES : (k + 1) * LANES
            ]
    got[ROUNDS, z] = flat[...].astype(jnp.bfloat16)

    pl.semaphore_wait(barrier, n_grp - 1 + len(offsets))

    copies = []
    for dz in range(1, n_grp):
        copy = pltpu.make_async_remote_copy(
            src_ref=got.at[ROUNDS, z],
            dst_ref=got.at[ROUNDS, z],
            send_sem=grp_send.at[dz],
            recv_sem=grp_recv.at[z],
            device_id={"grp": lax.rem(z + dz, n_grp)},
            device_id_type=MESH,
        )
        copy.start()
        copies.append(copy)

    def pass_on(source, order):
        for at, d in enumerate(offsets):
            copy = pltpu.make_async_remote_copy(
                src_ref=got.at[ROUNDS, source],
                dst_ref=got.at[ROUNDS + d, source],
                send_sem=blk_send.at[order, at],
                recv_sem=blk_recv.at[ROUNDS + d, source],
                device_id={"blk": lax.rem(b - d + n_blk, n_blk)},
                device_id_type=MESH,
            )
            copy.start()
            copies.append(copy)

    pass_on(z, 0)

    masks = lane_masks()
    for i in range(per):
        squares = []
        for k in range(chunks):
            parts = []
            for c in range(chan):
                row = i * image_rows + c * chunks + k
                part = jnp.broadcast_to(flat[row : row + 1, :], (ROWS, LANES))
                own[row] = part
                parts.append(part * part)
            squares.append(channel_sum(parts))
        for layer, (roots, inverses) in enumerate(variance_roots(squares, chan, masks)):
            for k in range(chunks):
                at = (i * LAYERS + layer) * chunks + k
                root[at] = roots[k]
                inv[at] = inverses[k]

    def arrived(k, source, sem):
        pltpu.make_async_remote_copy(
            src_ref=got.at[k, source],
            dst_ref=got.at[k, source],
            send_sem=grp_send.at[0],
            recv_sem=sem,
            device_id={"grp": z},
            device_id_type=MESH,
        ).wait_recv()

    for dz in range(1, n_grp):
        source = lax.rem(z + dz, n_grp)
        arrived(ROUNDS, source, grp_recv.at[source])
        pass_on(source, dz)

    def one_unit(places, slot):
        for s, (k, source) in enumerate(places):
            wide[s * per * image_rows : (s + 1) * per * image_rows, :] = got[
                k, source
            ].astype(jnp.float32)
        theirs = [
            [wide[pl.ds(c * chunks + j, ROWS, stride=image_rows), :] for c in range(chan)]
            for j in range(chunks)
        ]
        layers = variance_roots(
            [channel_sum([x * x for x in parts]) for parts in theirs], chan, masks
        )
        for i in range(per):
            cov = [
                channel_sum(
                    [own[i * image_rows + c * chunks + j] * theirs[j][c] for c in range(chan)]
                )
                for j in range(chunks)
            ]
            factor = 1.0 / (9 * chan)
            for layer in range(LAYERS):
                at = (i * LAYERS + layer) * chunks
                roots, inverses = layers[layer]
                cov = [x * factor + BIAS for x in stencil_sum(cov, masks)]
                cov = [
                    twice_relu(cov[j], root[at + j] * roots[j], inv[at + j] * inverses[j])
                    for j in range(chunks)
                ]
                factor = 1.0 / 9
            res[i, slot] = channel_sum(cov)

    def step(t, carry):
        home = ((t >= 1) & (t <= units)).astype(jnp.int32)
        away = 1 - home
        order = jnp.where(t > units, t - units, 0)
        source = lax.rem(z + order, n_grp)

        @pl.when(home == 0)
        def _():
            for d in offsets:
                arrived(ROUNDS + d, source, blk_recv.at[ROUNDS + d, source])

        unit = home * (t - 1)
        one_unit(
            [
                (ROUNDS + away * d, away * source + home * (unit * sources + s))
                for s, d in enumerate(offsets)
            ],
            home * unit + away * (units + source),
        )
        return carry

    lax.fori_loop(0, units + n_grp, step, 0)

    row = lax.broadcasted_iota(jnp.int32, (ROWS, LANES), 0)
    lane = lax.broadcasted_iota(jnp.int32, (ROWS, LANES), 1)
    for i in range(per):
        sums = [
            jnp.sum(res[i, slot], axis=1, keepdims=True) * (1.0 / pix)
            for slot in range(units + n_grp)
        ]
        home = jnp.zeros((ROWS, LANES), jnp.float32)
        for unit in range(units):
            home = jnp.where(lane == row + unit * ROWS, sums[unit], home)
        out[ROUNDS, i : i + 1, :] = jnp.sum(home, axis=0, keepdims=True)[:, :block]
        away = jnp.zeros((ROWS, LANES), jnp.float32)
        for source in range(n_grp):
            mine = (lane // per == source) & (lane % per == row % per)
            away = jnp.where(mine, sums[units + source], away)
        total = away
        for r in range(1, per):
            total = total + pltpu.roll(away, ROWS - r, 0)
        for at, d in enumerate(offsets):
            out[ROUNDS + d, i : i + 1, :] = total[at * per : at * per + 1, :block]
    for copy in copies:
        copy.wait_send()


def per_device(n_blk, n_grp, images):
    per, chan, pix = images.shape
    chunks = pix // LANES
    rows = per * chan * chunks
    block = per * n_grp
    assert block % ROWS == 0 and per * (SPAN - 1) == ROWS
    maps = per * LAYERS * chunks
    window = pl.pallas_call(
        functools.partial(kernel, n_blk, n_grp),
        out_shape=jax.ShapeDtypeStruct((SPAN, per, block), jnp.float32),
        in_specs=[pl.BlockSpec(memory_space=pltpu.HBM)],
        out_specs=pl.BlockSpec(memory_space=pltpu.VMEM),
        scratch_shapes=[
            pltpu.VMEM((chan, per, pix), jnp.bfloat16),
            pltpu.VMEM((SPAN, n_grp, rows, LANES), jnp.bfloat16),
            pltpu.VMEM((rows, ROWS, LANES), jnp.float32),
            pltpu.VMEM((rows, LANES), jnp.float32),
            pltpu.VMEM((maps, ROWS, LANES), jnp.float32),
            pltpu.VMEM((maps, ROWS, LANES), jnp.float32),
            pltpu.VMEM((ROWS * chan * chunks, LANES), jnp.float32),
            pltpu.VMEM((per, block // ROWS + n_grp, ROWS, LANES), jnp.float32),
            pltpu.SemaphoreType.DMA,
            pltpu.SemaphoreType.DMA((n_grp,)),
            pltpu.SemaphoreType.DMA((n_grp,)),
            pltpu.SemaphoreType.DMA((n_grp, SPAN - 1)),
            pltpu.SemaphoreType.DMA((SPAN, n_grp)),
        ],
        compiler_params=pltpu.CompilerParams(
            collective_id=0, has_side_effects=True, vmem_limit_bytes=32 * 1024 * 1024
        ),
    )(jnp.transpose(images, (1, 0, 2)))
    return jnp.transpose(window, (1, 0, 2))


def solution(mesh):
    spec = P(("blk", "grp"), None, None)
    body = functools.partial(per_device, mesh.shape["blk"], mesh.shape["grp"])
    return jax.shard_map(body, mesh=mesh, in_specs=(spec,), out_specs=spec, check_vma=False)
```

```python
import functools

import jax
import jax.numpy as jnp
from jax import lax
from jax.experimental import pallas as pl
from jax.experimental.pallas import tpu as pltpu
from jax.sharding import PartitionSpec as P

SIDE = 32
LAYERS = 3
ROUNDS = 2
SPAN = 2 * ROUNDS + 1
LANES = 128
ROWS = 8
BIAS = 0.1
BELOW_ONE = 1.0 - 2.0**-24
MESH = pl.DeviceIdType.MESH

ARC = (
    0.3183098449892848,
    -0.02253203775558662,
    0.005946535585369838,
    -0.002275705294168609,
    0.0008254564785290766,
    -0.00016869743862866002,
)


def stencil_sum(groups, masks):
    first, last, not_left, not_right = masks
    tall = []
    for maps in groups:
        above = jnp.where(first, 0.0, pltpu.roll(maps[-1], SIDE, 1))
        below = jnp.where(last, 0.0, pltpu.roll(maps[0], LANES - SIDE, 1))
        column = [above] + list(maps) + [below]
        pairs = [x + y for x, y in zip(column[:-1], column[1:])]
        tall.append([pairs[k] + column[k + 2] for k in range(len(maps))])
    out = []
    for maps in tall:
        left = [jnp.where(not_left, pltpu.roll(x, 1, 1), 0.0) for x in maps]
        right = [jnp.where(not_right, pltpu.roll(x, LANES - 1, 1), 0.0) for x in maps]
        out.append([x + (y + z) for x, y, z in zip(maps, left, right)])
    return out


def lane_masks():
    lane = lax.broadcasted_iota(jnp.int32, (ROWS, LANES), 1)
    col = lane % SIDE
    return lane < SIDE, lane >= LANES - SIDE, col != 0, col != SIDE - 1


def channel_sum(terms):
    total = terms[0]
    for term in terms[1:]:
        total = total + term
    return total


def affine(groups, factor):
    return [[x * factor + BIAS for x in maps] for maps in groups]


def roots_of(maps):
    inverse = [lax.rsqrt(x) for x in maps]
    return [x * y for x, y in zip(maps, inverse)], inverse


def twice_relu(cov, scale, inverse):
    a = jnp.minimum(jnp.abs(cov) * inverse, BELOW_ONE)
    y = 1.0 - a
    poly = ARC[-1]
    for c in ARC[-2::-1]:
        poly = poly * a + c
    bent = y * y * lax.rsqrt(y) * poly
    return scale * bent + jnp.minimum(jnp.maximum(cov, 0.0), scale)


def kernel(
    n_blk, n_grp, images, out, raw, turn, got, own, flat, root, inv, wide, res,
    raw_sem, grp_send, grp_recv, blk_send, blk_recv,
):
    b, z = lax.axis_index("blk"), lax.axis_index("grp")
    chan, per, pix = images.shape
    chunks = pix // LANES
    image_rows = chan * chunks
    block = per * n_grp
    units = block // ROWS
    sources = ROWS // per
    offsets = [d for d in range(-ROUNDS, ROUNDS + 1) if d]

    load = pltpu.make_async_copy(images, raw, raw_sem)
    load.start()
    barrier = pltpu.get_barrier_semaphore()
    for dz in range(1, n_grp):
        pl.semaphore_signal(
            barrier, inc=1, device_id={"grp": lax.rem(z + dz, n_grp)}, device_id_type=MESH
        )
    for d in offsets:
        pl.semaphore_signal(
            barrier, inc=1, device_id={"blk": lax.rem(b + d + n_blk, n_blk)}, device_id_type=MESH
        )
    load.wait()

    data = raw[...].astype(jnp.float32)
    for k in range(chunks):
        for c in range(chan):
            turn[pl.ds(k * ROWS + c, per, stride=chan), :] = data[
                c, :, k * LANES : (k + 1) * LANES
            ]
    lane = lax.broadcasted_iota(jnp.int32, (ROWS, LANES), 1)
    natural = [turn[k * ROWS : (k + 1) * ROWS, :] for k in range(chunks)]
    fold = LANES // SIDE
    for k in range(chunks):
        row = None
        for g in range(fold):
            at = g * chunks + k
            part = natural[at // fold]
            shift = (g - at % fold) * SIDE % LANES
            part = pltpu.roll(part, shift, 1) if shift else part
            row = part if row is None else jnp.where(lane >= g * SIDE, part, row)
        flat[pl.ds(k, per * chan, stride=chunks), :] = row[: per * chan]
    got[ROUNDS, z] = flat[...].astype(jnp.bfloat16)

    pl.semaphore_wait(barrier, n_grp - 1 + len(offsets))

    copies = []
    for dz in range(1, n_grp):
        copy = pltpu.make_async_remote_copy(
            src_ref=got.at[ROUNDS, z],
            dst_ref=got.at[ROUNDS, z],
            send_sem=grp_send.at[dz],
            recv_sem=grp_recv.at[z],
            device_id={"grp": lax.rem(z + dz, n_grp)},
            device_id_type=MESH,
        )
        copy.start()
        copies.append(copy)

    def pass_on(source, order):
        for at, d in enumerate(offsets):
            copy = pltpu.make_async_remote_copy(
                src_ref=got.at[ROUNDS, source],
                dst_ref=got.at[ROUNDS + d, source],
                send_sem=blk_send.at[order, at],
                recv_sem=blk_recv.at[ROUNDS + d, source],
                device_id={"blk": lax.rem(b - d + n_blk, n_blk)},
                device_id_type=MESH,
            )
            copy.start()
            copies.append(copy)

    pass_on(z, 0)

    masks = lane_masks()
    current = []
    for i in range(per):
        squares = []
        for k in range(chunks):
            parts = []
            for c in range(chan):
                row = i * image_rows + c * chunks + k
                part = jnp.broadcast_to(flat[row : row + 1, :], (ROWS, LANES))
                own[row] = part
                parts.append(part * part)
            squares.append(channel_sum(parts))
        current.append(squares)
    for layer in range(LAYERS):
        factor = 1.0 / 9 if layer else 1.0 / (9 * chan)
        current = affine(stencil_sum(current, masks), factor)
        for i in range(per):
            roots, inverses = roots_of(current[i])
            for k in range(chunks):
                at = (i * LAYERS + layer) * chunks + k
                root[at] = roots[k]
                inv[at] = inverses[k]

    def arrived(k, source, sem):
        pltpu.make_async_remote_copy(
            src_ref=got.at[k, source],
            dst_ref=got.at[k, source],
            send_sem=grp_send.at[0],
            recv_sem=sem,
            device_id={"grp": z},
            device_id_type=MESH,
        ).wait_recv()

    for dz in range(1, n_grp):
        source = lax.rem(z + dz, n_grp)
        arrived(ROUNDS, source, grp_recv.at[source])
        pass_on(source, dz)

    def work(members):
        maps = []
        for m, (places, slot) in enumerate(members):
            for s, (k, source) in enumerate(places):
                wide[m, s * per * image_rows : (s + 1) * per * image_rows, :] = got[
                    k, source
                ].astype(jnp.float32)
            theirs = [
                [wide[m, pl.ds(c * chunks + j, ROWS, stride=image_rows), :] for c in range(chan)]
                for j in range(chunks)
            ]
            maps.append([channel_sum([x * x for x in parts]) for parts in theirs])
            for i in range(per):
                maps.append(
                    [
                        channel_sum(
                            [
                                own[i * image_rows + c * chunks + j] * theirs[j][c]
                                for c in range(chan)
                            ]
                        )
                        for j in range(chunks)
                    ]
                )
        for layer in range(LAYERS):
            factor = 1.0 / 9 if layer else 1.0 / (9 * chan)
            maps = affine(stencil_sum(maps, masks), factor)
            for m in range(len(members)):
                roots, inverses = roots_of(maps[m * (per + 1)])
                for i in range(per):
                    at = (i * LAYERS + layer) * chunks
                    cov = maps[m * (per + 1) + 1 + i]
                    maps[m * (per + 1) + 1 + i] = [
                        twice_relu(cov[j], root[at + j] * roots[j], inv[at + j] * inverses[j])
                        for j in range(chunks)
                    ]
        for m, (places, slot) in enumerate(members):
            for i in range(per):
                res[i, slot] = channel_sum(maps[m * (per + 1) + 1 + i])

    def member(t):
        home = jnp.int32((t >= 1) & (t <= units))
        away = 1 - home
        order = jnp.where(t > units, t - units, 0)
        source = lax.rem(z + order, n_grp)

        @pl.when(home == 0)
        def _():
            for d in offsets:
                arrived(ROUNDS + d, source, blk_recv.at[ROUNDS + d, source])

        unit = home * (t - 1)
        places = [
            (ROUNDS + away * d, away * source + home * (unit * sources + s))
            for s, d in enumerate(offsets)
        ]
        return places, home * unit + away * (units + source)

    total_units = units + n_grp

    def step(t, carry):
        work([member(2 * t), member(2 * t + 1)])
        return carry

    lax.fori_loop(0, total_units // 2, step, 0)
    if total_units % 2:
        work([member(jnp.int32(total_units - 1))])

    row = lax.broadcasted_iota(jnp.int32, (ROWS, LANES), 0)
    lane = lax.broadcasted_iota(jnp.int32, (ROWS, LANES), 1)
    for i in range(per):
        sums = [
            jnp.sum(res[i, slot], axis=1, keepdims=True) * (1.0 / pix)
            for slot in range(units + n_grp)
        ]
        home = jnp.zeros((ROWS, LANES), jnp.float32)
        for unit in range(units):
            home = jnp.where(lane == row + unit * ROWS, sums[unit], home)
        out[ROUNDS, i : i + 1, :] = jnp.sum(home, axis=0, keepdims=True)[:, :block]
        away = jnp.zeros((ROWS, LANES), jnp.float32)
        for source in range(n_grp):
            mine = (lane // per == source) & (lane % per == row % per)
            away = jnp.where(mine, sums[units + source], away)
        total = away
        for r in range(1, per):
            total = total + pltpu.roll(away, ROWS - r, 0)
        for at, d in enumerate(offsets):
            out[ROUNDS + d, i : i + 1, :] = total[at * per : at * per + 1, :block]
    for copy in copies:
        copy.wait_send()


def per_device(n_blk, n_grp, images):
    per, chan, pix = images.shape
    chunks = pix // LANES
    rows = per * chan * chunks
    block = per * n_grp
    assert block % ROWS == 0 and per * (SPAN - 1) == ROWS
    maps = per * LAYERS * chunks
    window = pl.pallas_call(
        functools.partial(kernel, n_blk, n_grp),
        out_shape=jax.ShapeDtypeStruct((SPAN, per, block), jnp.float32),
        in_specs=[pl.BlockSpec(memory_space=pltpu.HBM)],
        out_specs=pl.BlockSpec(memory_space=pltpu.VMEM),
        scratch_shapes=[
            pltpu.VMEM((chan, per, pix), jnp.bfloat16),
            pltpu.VMEM((chunks * ROWS, LANES), jnp.float32),
            pltpu.VMEM((SPAN, n_grp, rows, LANES), jnp.bfloat16),
            pltpu.VMEM((rows, ROWS, LANES), jnp.float32),
            pltpu.VMEM((rows, LANES), jnp.float32),
            pltpu.VMEM((maps, ROWS, LANES), jnp.float32),
            pltpu.VMEM((maps, ROWS, LANES), jnp.float32),
            pltpu.VMEM((2, ROWS * chan * chunks, LANES), jnp.float32),
            pltpu.VMEM((per, block // ROWS + n_grp, ROWS, LANES), jnp.float32),
            pltpu.SemaphoreType.DMA,
            pltpu.SemaphoreType.DMA((n_grp,)),
            pltpu.SemaphoreType.DMA((n_grp,)),
            pltpu.SemaphoreType.DMA((n_grp, SPAN - 1)),
            pltpu.SemaphoreType.DMA((SPAN, n_grp)),
        ],
        compiler_params=pltpu.CompilerParams(
            collective_id=0, has_side_effects=True, vmem_limit_bytes=32 * 1024 * 1024
        ),
    )(jnp.transpose(images, (1, 0, 2)))
    return jnp.transpose(window, (1, 0, 2))


def solution(mesh):
    spec = P(("blk", "grp"), None, None)
    body = functools.partial(per_device, mesh.shape["blk"], mesh.shape["grp"])
    return jax.shard_map(body, mesh=mesh, in_specs=(spec,), out_specs=spec, check_vma=False)
```

```python
import functools

import jax
import jax.numpy as jnp
from jax import lax
from jax.experimental import pallas as pl
from jax.experimental.pallas import tpu as pltpu
from jax.sharding import PartitionSpec as P

SIDE = 32
LAYERS = 3
ROUNDS = 2
SPAN = 2 * ROUNDS + 1
LANES = 128
ROWS = 8
BIAS = 0.1
BELOW_ONE = 1.0 - 2.0**-24
MESH = pl.DeviceIdType.MESH

ARC = (
    0.3183098449892848,
    -0.02253203775558662,
    0.005946535585369838,
    -0.002275705294168609,
    0.0008254564785290766,
    -0.00016869743862866002,
)


def stencil_sum(groups, masks):
    first, last, not_left, not_right = masks
    tall = []
    for maps in groups:
        above = jnp.where(first, 0.0, pltpu.roll(maps[-1], SIDE, 1))
        below = jnp.where(last, 0.0, pltpu.roll(maps[0], LANES - SIDE, 1))
        column = [above] + list(maps) + [below]
        pairs = [x + y for x, y in zip(column[:-1], column[1:])]
        tall.append([pairs[k] + column[k + 2] for k in range(len(maps))])
    out = []
    for maps in tall:
        left = [jnp.where(not_left, pltpu.roll(x, 1, 1), 0.0) for x in maps]
        right = [jnp.where(not_right, pltpu.roll(x, LANES - 1, 1), 0.0) for x in maps]
        out.append([x + (y + z) for x, y, z in zip(maps, left, right)])
    return out


def lane_masks():
    lane = lax.broadcasted_iota(jnp.int32, (ROWS, LANES), 1)
    col = lane % SIDE
    return lane < SIDE, lane >= LANES - SIDE, col != 0, col != SIDE - 1


def channel_sum(terms):
    total = terms[0]
    for term in terms[1:]:
        total = total + term
    return total


def affine(groups, factor):
    return [[x * factor + BIAS for x in maps] for maps in groups]


def roots_of(maps):
    inverse = [lax.rsqrt(x) for x in maps]
    return [x * y for x, y in zip(maps, inverse)], inverse


def twice_relu(cov, scale, inverse):
    a = jnp.minimum(jnp.abs(cov) * inverse, BELOW_ONE)
    y = 1.0 - a
    poly = ARC[-1]
    for c in ARC[-2::-1]:
        poly = poly * a + c
    bent = y * y * lax.rsqrt(y) * poly
    return scale * bent + jnp.minimum(jnp.maximum(cov, 0.0), scale)


def kernel(
    n_blk, n_grp, images, out, raw, turn, got, own, flat, root, inv, wide,
    gone, back, raw_sem, grp_send, grp_recv, blk_send, blk_recv, gone_sem, back_sem,
):
    b, z = lax.axis_index("blk"), lax.axis_index("grp")
    chan, per, pix = images.shape
    chunks = pix // LANES
    image_rows = chan * chunks
    block = per * n_grp
    units = block // ROWS
    sources = ROWS // per
    span = range(1, ROUNDS + 1)

    load = pltpu.make_async_copy(images, raw, raw_sem)
    load.start()
    barrier = pltpu.get_barrier_semaphore()
    for dz in range(1, n_grp):
        pl.semaphore_signal(
            barrier, inc=1, device_id={"grp": lax.rem(z + dz, n_grp)}, device_id_type=MESH
        )
    for d in span:
        pl.semaphore_signal(
            barrier, inc=1, device_id={"blk": lax.rem(b - d + n_blk, n_blk)}, device_id_type=MESH
        )
    load.wait()

    data = raw[...].astype(jnp.float32)
    for k in range(chunks):
        for c in range(chan):
            turn[pl.ds(k * ROWS + c, per, stride=chan), :] = data[
                c, :, k * LANES : (k + 1) * LANES
            ]
    lane = lax.broadcasted_iota(jnp.int32, (ROWS, LANES), 1)
    natural = [turn[k * ROWS : (k + 1) * ROWS, :] for k in range(chunks)]
    fold = LANES // SIDE
    for k in range(chunks):
        row = None
        for g in range(fold):
            at = g * chunks + k
            part = natural[at // fold]
            shift = (g - at % fold) * SIDE % LANES
            part = pltpu.roll(part, shift, 1) if shift else part
            row = part if row is None else jnp.where(lane >= g * SIDE, part, row)
        flat[pl.ds(k, per * chan, stride=chunks), :] = row[: per * chan]
    got[0, z] = flat[...].astype(jnp.bfloat16)

    pl.semaphore_wait(barrier, n_grp - 1 + ROUNDS)

    copies = []
    for dz in range(1, n_grp):
        copy = pltpu.make_async_remote_copy(
            src_ref=got.at[0, z],
            dst_ref=got.at[0, z],
            send_sem=grp_send.at[dz],
            recv_sem=grp_recv.at[z],
            device_id={"grp": lax.rem(z + dz, n_grp)},
            device_id_type=MESH,
        )
        copy.start()
        copies.append(copy)

    def pass_on(source, order):
        for d in span:
            copy = pltpu.make_async_remote_copy(
                src_ref=got.at[0, source],
                dst_ref=got.at[d, source],
                send_sem=blk_send.at[order, d - 1],
                recv_sem=blk_recv.at[d - 1, source],
                device_id={"blk": lax.rem(b + d, n_blk)},
                device_id_type=MESH,
            )
            copy.start()
            copies.append(copy)

    pass_on(z, 0)

    masks = lane_masks()
    current = []
    for i in range(per):
        squares = []
        for k in range(chunks):
            parts = []
            for c in range(chan):
                row = i * image_rows + c * chunks + k
                part = jnp.broadcast_to(flat[row : row + 1, :], (ROWS, LANES))
                own[row] = part
                parts.append(part * part)
            squares.append(channel_sum(parts))
        current.append(squares)
    for layer in range(LAYERS):
        factor = 1.0 / 9 if layer else 1.0 / (9 * chan)
        current = affine(stencil_sum(current, masks), factor)
        for i in range(per):
            roots, inverses = roots_of(current[i])
            for k in range(chunks):
                at = (i * LAYERS + layer) * chunks + k
                root[at] = roots[k]
                inv[at] = inverses[k]

    def arrived(ref, sem):
        pltpu.make_async_remote_copy(
            src_ref=ref,
            dst_ref=ref,
            send_sem=grp_send.at[0],
            recv_sem=sem,
            device_id={"grp": z},
            device_id_type=MESH,
        ).wait_recv()

    for dz in range(1, n_grp):
        source = lax.rem(z + dz, n_grp)
        arrived(got.at[0, source], grp_recv.at[source])
        pass_on(source, dz)

    def work(members):
        maps = []
        for m, places in enumerate(members):
            for s, (k, source) in enumerate(places):
                wide[m, s * per * image_rows : (s + 1) * per * image_rows, :] = got[
                    k, source
                ].astype(jnp.float32)
            theirs = [
                [wide[m, pl.ds(c * chunks + j, ROWS, stride=image_rows), :] for c in range(chan)]
                for j in range(chunks)
            ]
            maps.append([channel_sum([x * x for x in parts]) for parts in theirs])
            for i in range(per):
                maps.append(
                    [
                        channel_sum(
                            [
                                own[i * image_rows + c * chunks + j] * theirs[j][c]
                                for c in range(chan)
                            ]
                        )
                        for j in range(chunks)
                    ]
                )
        for layer in range(LAYERS):
            factor = 1.0 / 9 if layer else 1.0 / (9 * chan)
            maps = affine(stencil_sum(maps, masks), factor)
            for m in range(len(members)):
                roots, inverses = roots_of(maps[m * (per + 1)])
                for i in range(per):
                    at = (i * LAYERS + layer) * chunks
                    cov = maps[m * (per + 1) + 1 + i]
                    maps[m * (per + 1) + 1 + i] = [
                        twice_relu(cov[j], root[at + j] * roots[j], inv[at + j] * inverses[j])
                        for j in range(chunks)
                    ]
        return [
            [
                jnp.sum(channel_sum(maps[m * (per + 1) + 1 + i]), axis=1, keepdims=True)
                * (1.0 / pix)
                for i in range(per)
            ]
            for m in range(len(members))
        ]

    row = lax.broadcasted_iota(jnp.int32, (ROWS, LANES), 0)

    home = [jnp.zeros((ROWS, LANES), jnp.float32) for _ in range(per)]
    for unit in range(units):
        (sums,) = work([[(0, unit * sources + s) for s in range(sources)]])
        for i in range(per):
            home[i] = jnp.where(lane == row + unit * ROWS, sums[i], home[i])
    for i in range(per):
        out[ROUNDS, i : i + 1, :] = jnp.sum(home[i], axis=0, keepdims=True)[:, :block]

    step = sources // ROUNDS
    before = [jnp.zeros((ROWS, LANES), jnp.float32) for _ in range(per)]
    for first in range(0, n_grp, step):
        places = []
        for a in range(step):
            source = lax.rem(z + first + a, n_grp)
            for d in span:
                arrived(got.at[d, source], blk_recv.at[d - 1, source])
                places.append((d, source))
        (sums,) = work([places])
        mirror = jnp.zeros((ROWS, LANES), jnp.float32)
        for i in range(per):
            mirror = jnp.where(lane == z * per + i, sums[i], mirror)
        for s, (d, source) in enumerate(places):
            at = first // step * sources + s
            gone[at] = mirror[s * per : (s + 1) * per, :]
            copy = pltpu.make_async_remote_copy(
                src_ref=gone.at[at],
                dst_ref=back.at[d - 1, z],
                send_sem=gone_sem.at[at],
                recv_sem=back_sem.at[d - 1, z],
                device_id={"blk": lax.rem(b - d + n_blk, n_blk), "grp": source},
                device_id_type=MESH,
            )
            copy.start()
            copies.append(copy)
        column = lax.rem(row, per) + per * lax.rem(z + first + row // (per * ROUNDS), n_grp)
        for i in range(per):
            before[i] = jnp.where(lane == column, sums[i], before[i])
    place = lax.rem(row // per, ROUNDS)
    for d in span:
        for i in range(per):
            mine = jnp.where(place == d - 1, before[i], 0.0)
            out[ROUNDS - d, i : i + 1, :] = jnp.sum(mine, axis=0, keepdims=True)[:, :block]

    for d in span:
        for source in range(n_grp):
            arrived(back.at[d - 1, source], back_sem.at[d - 1, source])
        total = channel_sum([back[d - 1, source] for source in range(n_grp)])
        out[ROUNDS + d] = total[:, :block]
    for copy in copies:
        copy.wait_send()


def per_device(n_blk, n_grp, images):
    per, chan, pix = images.shape
    chunks = pix // LANES
    rows = per * chan * chunks
    block = per * n_grp
    assert block % ROWS == 0 and ROWS % (per * ROUNDS) == 0
    sources = ROWS // per
    assert n_grp % (sources // ROUNDS) == 0
    maps = per * LAYERS * chunks
    window = pl.pallas_call(
        functools.partial(kernel, n_blk, n_grp),
        out_shape=jax.ShapeDtypeStruct((SPAN, per, block), jnp.float32),
        in_specs=[pl.BlockSpec(memory_space=pltpu.HBM)],
        out_specs=pl.BlockSpec(memory_space=pltpu.VMEM),
        scratch_shapes=[
            pltpu.VMEM((chan, per, pix), jnp.bfloat16),
            pltpu.VMEM((chunks * ROWS, LANES), jnp.float32),
            pltpu.VMEM((ROUNDS + 1, n_grp, rows, LANES), jnp.bfloat16),
            pltpu.VMEM((rows, ROWS, LANES), jnp.float32),
            pltpu.VMEM((rows, LANES), jnp.float32),
            pltpu.VMEM((maps, ROWS, LANES), jnp.float32),
            pltpu.VMEM((maps, ROWS, LANES), jnp.float32),
            pltpu.VMEM((1, ROWS * chan * chunks, LANES), jnp.float32),
            pltpu.VMEM((ROUNDS * n_grp, per, LANES), jnp.float32),
            pltpu.VMEM((ROUNDS, n_grp, per, LANES), jnp.float32),
            pltpu.SemaphoreType.DMA,
            pltpu.SemaphoreType.DMA((n_grp,)),
            pltpu.SemaphoreType.DMA((n_grp,)),
            pltpu.SemaphoreType.DMA((n_grp, ROUNDS)),
            pltpu.SemaphoreType.DMA((ROUNDS, n_grp)),
            pltpu.SemaphoreType.DMA((ROUNDS * n_grp,)),
            pltpu.SemaphoreType.DMA((ROUNDS, n_grp)),
        ],
        compiler_params=pltpu.CompilerParams(
            collective_id=0, has_side_effects=True, vmem_limit_bytes=32 * 1024 * 1024
        ),
    )(jnp.transpose(images, (1, 0, 2)))
    return jnp.transpose(window, (1, 0, 2))


def solution(mesh):
    spec = P(("blk", "grp"), None, None)
    body = functools.partial(per_device, mesh.shape["blk"], mesh.shape["grp"])
    return jax.shard_map(body, mesh=mesh, in_specs=(spec,), out_specs=spec, check_vma=False)
```

```python
import functools

import jax
import jax.numpy as jnp
from jax import lax
from jax.experimental import pallas as pl
from jax.experimental.pallas import tpu as pltpu
from jax.sharding import PartitionSpec as P

SIDE = 32
LAYERS = 3
ROUNDS = 2
SPAN = 2 * ROUNDS + 1
LANES = 128
ROWS = 8
BIAS = 0.1
BELOW_ONE = 1.0 - 2.0**-24
MESH = pl.DeviceIdType.MESH

ARC = (
    0.3183098449892848,
    -0.02253203775558662,
    0.005946535585369838,
    -0.002275705294168609,
    0.0008254564785290766,
    -0.00016869743862866002,
)


def stencil_sum(groups, masks):
    first, last, not_left, not_right = masks
    tall = []
    for maps in groups:
        above = jnp.where(first, 0.0, pltpu.roll(maps[-1], SIDE, 1))
        below = jnp.where(last, 0.0, pltpu.roll(maps[0], LANES - SIDE, 1))
        column = [above] + list(maps) + [below]
        pairs = [x + y for x, y in zip(column[:-1], column[1:])]
        tall.append([pairs[k] + column[k + 2] for k in range(len(maps))])
    out = []
    for maps in tall:
        left = [jnp.where(not_left, pltpu.roll(x, 1, 1), 0.0) for x in maps]
        right = [jnp.where(not_right, pltpu.roll(x, LANES - 1, 1), 0.0) for x in maps]
        out.append([x + (y + z) for x, y, z in zip(maps, left, right)])
    return out


def lane_masks():
    lane = lax.broadcasted_iota(jnp.int32, (ROWS, LANES), 1)
    col = lane % SIDE
    return lane < SIDE, lane >= LANES - SIDE, col != 0, col != SIDE - 1


def channel_sum(terms):
    total = terms[0]
    for term in terms[1:]:
        total = total + term
    return total


def affine(groups, factor):
    return [[x * factor + BIAS for x in maps] for maps in groups]


def roots_of(maps):
    inverse = [lax.rsqrt(x) for x in maps]
    return [x * y for x, y in zip(maps, inverse)], inverse


def twice_relu(cov, scale, inverse):
    a = jnp.minimum(jnp.abs(cov) * inverse, BELOW_ONE)
    y = 1.0 - a
    poly = ARC[-1]
    for c in ARC[-2::-1]:
        poly = poly * a + c
    bent = y * y * lax.rsqrt(y) * poly
    return scale * bent + jnp.minimum(jnp.maximum(cov, 0.0), scale)


def kernel(
    n_blk, n_grp, images, out, raw, turn, got, own, flat, root, inv, wide, res,
    raw_sem, send, recv,
):
    b, z = lax.axis_index("blk"), lax.axis_index("grp")
    chan, per, pix = images.shape
    chunks = pix // LANES
    image_rows = chan * chunks
    block = per * n_grp
    units = block // ROWS
    sources = ROWS // per
    offsets = [d for d in range(-ROUNDS, ROUNDS + 1) if d]

    load = pltpu.make_async_copy(images, raw, raw_sem)
    load.start()
    barrier = pltpu.get_barrier_semaphore()
    def partner(dz, d):
        return {"blk": lax.rem(b + d + n_blk, n_blk), "grp": lax.rem(z + dz, n_grp)}

    partners = [(0, d) for d in offsets]
    partners += [(dz, d) for dz in range(1, n_grp) for d in [0] + offsets]
    for dz, d in partners:
        pl.semaphore_signal(barrier, inc=1, device_id=partner(dz, d), device_id_type=MESH)
    load.wait()

    data = raw[...].astype(jnp.float32)
    for k in range(chunks):
        for c in range(chan):
            turn[pl.ds(k * ROWS + c, per, stride=chan), :] = data[
                c, :, k * LANES : (k + 1) * LANES
            ]
    lane = lax.broadcasted_iota(jnp.int32, (ROWS, LANES), 1)
    natural = [turn[k * ROWS : (k + 1) * ROWS, :] for k in range(chunks)]
    fold = LANES // SIDE
    for k in range(chunks):
        row = None
        for g in range(fold):
            at = g * chunks + k
            part = natural[at // fold]
            shift = (g - at % fold) * SIDE % LANES
            part = pltpu.roll(part, shift, 1) if shift else part
            row = part if row is None else jnp.where(lane >= g * SIDE, part, row)
        flat[pl.ds(k, per * chan, stride=chunks), :] = row[: per * chan]
    got[ROUNDS, z] = flat[...].astype(jnp.bfloat16)

    pl.semaphore_wait(barrier, len(partners))

    copies = []
    for dz, d in partners:
        copy = pltpu.make_async_remote_copy(
            src_ref=got.at[ROUNDS, z],
            dst_ref=got.at[ROUNDS - d, z],
            send_sem=send.at[dz, ROUNDS + d],
            recv_sem=recv.at[ROUNDS - d, z],
            device_id=partner(dz, d),
            device_id_type=MESH,
        )
        copy.start()
        copies.append(copy)

    masks = lane_masks()
    current = []
    for i in range(per):
        squares = []
        for k in range(chunks):
            parts = []
            for c in range(chan):
                row = i * image_rows + c * chunks + k
                part = jnp.broadcast_to(flat[row : row + 1, :], (ROWS, LANES))
                own[row] = part
                parts.append(part * part)
            squares.append(channel_sum(parts))
        current.append(squares)
    for layer in range(LAYERS):
        factor = 1.0 / 9 if layer else 1.0 / (9 * chan)
        current = affine(stencil_sum(current, masks), factor)
        for i in range(per):
            roots, inverses = roots_of(current[i])
            for k in range(chunks):
                at = (i * LAYERS + layer) * chunks + k
                root[at] = roots[k]
                inv[at] = inverses[k]

    def arrived(k, source):
        pltpu.make_async_remote_copy(
            src_ref=got.at[k, source],
            dst_ref=got.at[k, source],
            send_sem=send.at[0, 0],
            recv_sem=recv.at[k, source],
            device_id={"grp": z},
            device_id_type=MESH,
        ).wait_recv()

    def work(members):
        maps = []
        for m, (places, slot) in enumerate(members):
            for s, (k, source) in enumerate(places):
                wide[m, s * per * image_rows : (s + 1) * per * image_rows, :] = got[
                    k, source
                ].astype(jnp.float32)
            theirs = [
                [wide[m, pl.ds(c * chunks + j, ROWS, stride=image_rows), :] for c in range(chan)]
                for j in range(chunks)
            ]
            maps.append([channel_sum([x * x for x in parts]) for parts in theirs])
            for i in range(per):
                maps.append(
                    [
                        channel_sum(
                            [
                                own[i * image_rows + c * chunks + j] * theirs[j][c]
                                for c in range(chan)
                            ]
                        )
                        for j in range(chunks)
                    ]
                )
        for layer in range(LAYERS):
            factor = 1.0 / 9 if layer else 1.0 / (9 * chan)
            maps = affine(stencil_sum(maps, masks), factor)
            for m in range(len(members)):
                roots, inverses = roots_of(maps[m * (per + 1)])
                for i in range(per):
                    at = (i * LAYERS + layer) * chunks
                    cov = maps[m * (per + 1) + 1 + i]
                    maps[m * (per + 1) + 1 + i] = [
                        twice_relu(cov[j], root[at + j] * roots[j], inv[at + j] * inverses[j])
                        for j in range(chunks)
                    ]
        for m, (places, slot) in enumerate(members):
            for i in range(per):
                res[i, slot] = channel_sum(maps[m * (per + 1) + 1 + i])

    def member(t):
        home = jnp.int32((t >= 1) & (t <= units))
        away = 1 - home
        order = jnp.where(t > units, t - units, 0)
        source = lax.rem(z + order, n_grp)

        @pl.when(home == 0)
        def _():
            for d in offsets:
                arrived(ROUNDS + d, source)

        @pl.when(t == 1)
        def _():
            for dz in range(1, n_grp):
                arrived(ROUNDS, lax.rem(z + dz, n_grp))

        unit = home * (t - 1)
        places = [
            (ROUNDS + away * d, away * source + home * (unit * sources + s))
            for s, d in enumerate(offsets)
        ]
        return places, home * unit + away * (units + source)

    total_units = units + n_grp

    def step(t, carry):
        work([member(2 * t), member(2 * t + 1)])
        return carry

    lax.fori_loop(0, total_units // 2, step, 0)
    if total_units % 2:
        work([member(jnp.int32(total_units - 1))])

    row = lax.broadcasted_iota(jnp.int32, (ROWS, LANES), 0)
    lane = lax.broadcasted_iota(jnp.int32, (ROWS, LANES), 1)
    for i in range(per):
        sums = [
            jnp.sum(res[i, slot], axis=1, keepdims=True) * (1.0 / pix)
            for slot in range(units + n_grp)
        ]
        home = jnp.zeros((ROWS, LANES), jnp.float32)
        for unit in range(units):
            home = jnp.where(lane == row + unit * ROWS, sums[unit], home)
        out[ROUNDS, i : i + 1, :] = jnp.sum(home, axis=0, keepdims=True)[:, :block]
        away = jnp.zeros((ROWS, LANES), jnp.float32)
        for source in range(n_grp):
            mine = (lane // per == source) & (lane % per == row % per)
            away = jnp.where(mine, sums[units + source], away)
        total = away
        for r in range(1, per):
            total = total + pltpu.roll(away, ROWS - r, 0)
        for at, d in enumerate(offsets):
            out[ROUNDS + d, i : i + 1, :] = total[at * per : at * per + 1, :block]
    for copy in copies:
        copy.wait_send()


def per_device(n_blk, n_grp, images):
    per, chan, pix = images.shape
    chunks = pix // LANES
    rows = per * chan * chunks
    block = per * n_grp
    assert block % ROWS == 0 and per * (SPAN - 1) == ROWS
    maps = per * LAYERS * chunks
    window = pl.pallas_call(
        functools.partial(kernel, n_blk, n_grp),
        out_shape=jax.ShapeDtypeStruct((SPAN, per, block), jnp.float32),
        in_specs=[pl.BlockSpec(memory_space=pltpu.HBM)],
        out_specs=pl.BlockSpec(memory_space=pltpu.VMEM),
        scratch_shapes=[
            pltpu.VMEM((chan, per, pix), jnp.bfloat16),
            pltpu.VMEM((chunks * ROWS, LANES), jnp.float32),
            pltpu.VMEM((SPAN, n_grp, rows, LANES), jnp.bfloat16),
            pltpu.VMEM((rows, ROWS, LANES), jnp.float32),
            pltpu.VMEM((rows, LANES), jnp.float32),
            pltpu.VMEM((maps, ROWS, LANES), jnp.float32),
            pltpu.VMEM((maps, ROWS, LANES), jnp.float32),
            pltpu.VMEM((2, ROWS * chan * chunks, LANES), jnp.float32),
            pltpu.VMEM((per, block // ROWS + n_grp, ROWS, LANES), jnp.float32),
            pltpu.SemaphoreType.DMA,
            pltpu.SemaphoreType.DMA((n_grp, SPAN)),
            pltpu.SemaphoreType.DMA((SPAN, n_grp)),
        ],
        compiler_params=pltpu.CompilerParams(
            collective_id=0, has_side_effects=True, vmem_limit_bytes=32 * 1024 * 1024
        ),
    )(jnp.transpose(images, (1, 0, 2)))
    return jnp.transpose(window, (1, 0, 2))


def solution(mesh):
    spec = P(("blk", "grp"), None, None)
    body = functools.partial(per_device, mesh.shape["blk"], mesh.shape["grp"])
    return jax.shard_map(body, mesh=mesh, in_specs=(spec,), out_specs=spec, check_vma=False)
```

```python
import functools

import jax
import jax.numpy as jnp
from jax import lax
from jax.experimental import pallas as pl
from jax.experimental.pallas import tpu as pltpu
from jax.sharding import PartitionSpec as P

SIDE = 32
LAYERS = 3
ROUNDS = 2
SPAN = 2 * ROUNDS + 1
LANES = 128
ROWS = 8
BIAS = 0.1
BELOW_ONE = 1.0 - 2.0**-24
MESH = pl.DeviceIdType.MESH

ARC = (
    0.3183098449892848,
    -0.02253203775558662,
    0.005946535585369838,
    -0.002275705294168609,
    0.0008254564785290766,
    -0.00016869743862866002,
)


def stencil_sum(groups, masks):
    first, last, not_left, not_right = masks
    tall = []
    for maps in groups:
        above = jnp.where(first, 0.0, pltpu.roll(maps[-1], SIDE, 1))
        below = jnp.where(last, 0.0, pltpu.roll(maps[0], LANES - SIDE, 1))
        column = [above] + list(maps) + [below]
        pairs = [x + y for x, y in zip(column[:-1], column[1:])]
        tall.append([pairs[k] + column[k + 2] for k in range(len(maps))])
    out = []
    for maps in tall:
        left = [jnp.where(not_left, pltpu.roll(x, 1, 1), 0.0) for x in maps]
        right = [jnp.where(not_right, pltpu.roll(x, LANES - 1, 1), 0.0) for x in maps]
        out.append([x + (y + z) for x, y, z in zip(maps, left, right)])
    return out


def lane_masks():
    lane = lax.broadcasted_iota(jnp.int32, (ROWS, LANES), 1)
    col = lane % SIDE
    return lane < SIDE, lane >= LANES - SIDE, col != 0, col != SIDE - 1


def channel_sum(terms):
    total = terms[0]
    for term in terms[1:]:
        total = total + term
    return total


def affine(groups, factor):
    return [[x * factor + BIAS for x in maps] for maps in groups]


def roots_of(maps):
    inverse = [lax.rsqrt(x) for x in maps]
    return [x * y for x, y in zip(maps, inverse)], inverse


def twice_relu(cov, scale, inverse):
    a = jnp.minimum(jnp.abs(cov) * inverse, BELOW_ONE)
    y = 1.0 - a
    poly = ARC[-1]
    for c in ARC[-2::-1]:
        poly = poly * a + c
    bent = y * y * lax.rsqrt(y) * poly
    return scale * bent + jnp.minimum(jnp.maximum(cov, 0.0), scale)


def kernel(
    n_blk, n_grp, images, out, raw, turn, got, own, flat, root, inv, wide, res,
    raw_sem, grp_send, grp_recv, blk_send, blk_recv,
):
    b, z = lax.axis_index("blk"), lax.axis_index("grp")
    chan, per, pix = images.shape
    chunks = pix // LANES
    image_rows = chan * chunks
    block = per * n_grp
    units = block // ROWS
    sources = ROWS // per
    offsets = [d for d in range(-ROUNDS, ROUNDS + 1) if d]

    load = pltpu.make_async_copy(images, raw, raw_sem)
    load.start()
    barrier = pltpu.get_barrier_semaphore()
    for dz in range(1, n_grp):
        pl.semaphore_signal(
            barrier, inc=1, device_id={"grp": lax.rem(z + dz, n_grp)}, device_id_type=MESH
        )
    for d in offsets:
        pl.semaphore_signal(
            barrier, inc=1, device_id={"blk": lax.rem(b + d + n_blk, n_blk)}, device_id_type=MESH
        )
    load.wait()

    data = raw[...].astype(jnp.float32)
    for k in range(chunks):
        for c in range(chan):
            turn[pl.ds(k * ROWS + c, per, stride=chan), :] = data[
                c, :, k * LANES : (k + 1) * LANES
            ]
    lane = lax.broadcasted_iota(jnp.int32, (ROWS, LANES), 1)
    natural = [turn[k * ROWS : (k + 1) * ROWS, :] for k in range(chunks)]
    fold = LANES // SIDE
    for k in range(chunks):
        row = None
        for g in range(fold):
            at = g * chunks + k
            part = natural[at // fold]
            shift = (g - at % fold) * SIDE % LANES
            part = pltpu.roll(part, shift, 1) if shift else part
            row = part if row is None else jnp.where(lane >= g * SIDE, part, row)
        flat[pl.ds(k, per * chan, stride=chunks), :] = row[: per * chan]
    got[ROUNDS, z] = flat[...].astype(jnp.bfloat16)

    pl.semaphore_wait(barrier, n_grp - 1 + len(offsets))

    copies = []
    for dz in range(1, n_grp):
        copy = pltpu.make_async_remote_copy(
            src_ref=got.at[ROUNDS, z],
            dst_ref=got.at[ROUNDS, z],
            send_sem=grp_send.at[dz],
            recv_sem=grp_recv.at[z],
            device_id={"grp": lax.rem(z + dz, n_grp)},
            device_id_type=MESH,
        )
        copy.start()
        copies.append(copy)

    def pass_on(source, order):
        for at, d in enumerate(offsets):
            copy = pltpu.make_async_remote_copy(
                src_ref=got.at[ROUNDS, source],
                dst_ref=got.at[ROUNDS + d, source],
                send_sem=blk_send.at[order, at],
                recv_sem=blk_recv.at[ROUNDS + d, source],
                device_id={"blk": lax.rem(b - d + n_blk, n_blk)},
                device_id_type=MESH,
            )
            copy.start()
            copies.append(copy)

    pass_on(z, 0)

    masks = lane_masks()
    current = []
    for i in range(per):
        squares = []
        for k in range(chunks):
            parts = []
            for c in range(chan):
                row = i * image_rows + c * chunks + k
                part = jnp.broadcast_to(flat[row : row + 1, :], (ROWS, LANES))
                own[row] = part
                parts.append(part * part)
            squares.append(channel_sum(parts))
        current.append(squares)
    for layer in range(LAYERS):
        factor = 1.0 / 9 if layer else 1.0 / (9 * chan)
        current = affine(stencil_sum(current, masks), factor)
        for i in range(per):
            roots, inverses = roots_of(current[i])
            for k in range(chunks):
                at = (i * LAYERS + layer) * chunks + k
                root[at] = roots[k]
                inv[at] = inverses[k]

    def arrived(k, source, sem):
        pltpu.make_async_remote_copy(
            src_ref=got.at[k, source],
            dst_ref=got.at[k, source],
            send_sem=grp_send.at[0],
            recv_sem=sem,
            device_id={"grp": z},
            device_id_type=MESH,
        ).wait_recv()

    for dz in range(1, n_grp):
        source = lax.rem(z + dz, n_grp)
        arrived(ROUNDS, source, grp_recv.at[source])
        pass_on(source, dz)

    def work(members):
        maps = []
        for m, (places, slot) in enumerate(members):
            for s, (k, source) in enumerate(places):
                wide[m, s * per * image_rows : (s + 1) * per * image_rows, :] = got[
                    k, source
                ].astype(jnp.float32)
            theirs = [
                [wide[m, pl.ds(c * chunks + j, ROWS, stride=image_rows), :] for c in range(chan)]
                for j in range(chunks)
            ]
            maps.append([channel_sum([x * x for x in parts]) for parts in theirs])
            for i in range(per):
                maps.append(
                    [
                        channel_sum(
                            [
                                own[i * image_rows + c * chunks + j] * theirs[j][c]
                                for c in range(chan)
                            ]
                        )
                        for j in range(chunks)
                    ]
                )
        for layer in range(LAYERS):
            factor = 1.0 / 9 if layer else 1.0 / (9 * chan)
            maps = affine(stencil_sum(maps, masks), factor)
            for m in range(len(members)):
                roots, inverses = roots_of(maps[m * (per + 1)])
                for i in range(per):
                    at = (i * LAYERS + layer) * chunks
                    cov = maps[m * (per + 1) + 1 + i]
                    maps[m * (per + 1) + 1 + i] = [
                        twice_relu(cov[j], root[at + j] * roots[j], inv[at + j] * inverses[j])
                        for j in range(chunks)
                    ]
        for m, (places, slot) in enumerate(members):
            for i in range(per):
                res[i, slot] = channel_sum(maps[m * (per + 1) + 1 + i])

    def member(t):
        home = jnp.int32((t >= 1) & (t <= units))
        away = 1 - home
        order = jnp.where(t > units, t - units, 0)
        source = lax.rem(z + order, n_grp)

        @pl.when(home == 0)
        def _():
            for d in offsets:
                arrived(ROUNDS + d, source, blk_recv.at[ROUNDS + d, source])

        unit = home * (t - 1)
        places = [
            (ROUNDS + away * d, away * source + home * (unit * sources + s))
            for s, d in enumerate(offsets)
        ]
        return places, home * unit + away * (units + source)

    total_units = units + n_grp

    def step(t, carry):
        work([member(2 * t), member(2 * t + 1)])
        return carry

    lax.fori_loop(0, total_units // 2, step, 0)
    if total_units % 2:
        work([member(jnp.int32(total_units - 1))])

    row = lax.broadcasted_iota(jnp.int32, (ROWS, LANES), 0)
    lane = lax.broadcasted_iota(jnp.int32, (ROWS, LANES), 1)
    for i in range(per):
        sums = [
            jnp.sum(res[i, slot], axis=1, keepdims=True) * (1.0 / pix)
            for slot in range(units + n_grp)
        ]
        home = jnp.zeros((ROWS, LANES), jnp.float32)
        for unit in range(units):
            home = jnp.where(lane == row + unit * ROWS, sums[unit], home)
        out[ROUNDS, i : i + 1, :] = jnp.sum(home, axis=0, keepdims=True)[:, :block]
        away = jnp.zeros((ROWS, LANES), jnp.float32)
        for source in range(n_grp):
            mine = (lane // per == source) & (lane % per == row % per)
            away = jnp.where(mine, sums[units + source], away)
        total = away
        for r in range(1, per):
            total = total + pltpu.roll(away, ROWS - r, 0)
        for at, d in enumerate(offsets):
            out[ROUNDS + d, i : i + 1, :] = total[at * per : at * per + 1, :block]
    for copy in copies:
        copy.wait_send()


def per_device(n_blk, n_grp, images):
    per, chan, pix = images.shape
    chunks = pix // LANES
    rows = per * chan * chunks
    block = per * n_grp
    assert block % ROWS == 0 and per * (SPAN - 1) == ROWS
    maps = per * LAYERS * chunks
    window = pl.pallas_call(
        functools.partial(kernel, n_blk, n_grp),
        out_shape=jax.ShapeDtypeStruct((SPAN, per, block), jnp.float32),
        in_specs=[pl.BlockSpec(memory_space=pltpu.HBM)],
        out_specs=pl.BlockSpec(memory_space=pltpu.VMEM),
        scratch_shapes=[
            pltpu.VMEM((chan, per, pix), jnp.bfloat16),
            pltpu.VMEM((chunks * ROWS, LANES), jnp.float32),
            pltpu.VMEM((SPAN, n_grp, rows, LANES), jnp.bfloat16),
            pltpu.VMEM((rows, ROWS, LANES), jnp.float32),
            pltpu.VMEM((rows, LANES), jnp.float32),
            pltpu.VMEM((maps, ROWS, LANES), jnp.float32),
            pltpu.VMEM((maps, ROWS, LANES), jnp.float32),
            pltpu.VMEM((2, ROWS * chan * chunks, LANES), jnp.float32),
            pltpu.VMEM((per, block // ROWS + n_grp, ROWS, LANES), jnp.float32),
            pltpu.SemaphoreType.DMA,
            pltpu.SemaphoreType.DMA((n_grp,)),
            pltpu.SemaphoreType.DMA((n_grp,)),
            pltpu.SemaphoreType.DMA((n_grp, SPAN - 1)),
            pltpu.SemaphoreType.DMA((SPAN, n_grp)),
        ],
        compiler_params=pltpu.CompilerParams(
            collective_id=0, has_side_effects=True, vmem_limit_bytes=60 * 1024 * 1024
        ),
    )(jnp.transpose(images, (1, 0, 2)))
    return jnp.transpose(window, (1, 0, 2))


def solution(mesh):
    spec = P(("blk", "grp"), None, None)
    body = functools.partial(per_device, mesh.shape["blk"], mesh.shape["grp"])
    return jax.shard_map(body, mesh=mesh, in_specs=(spec,), out_specs=spec, check_vma=False)
```

```python
import functools

import jax
import jax.numpy as jnp
from jax import lax
from jax.experimental import pallas as pl
from jax.experimental.pallas import tpu as pltpu
from jax.sharding import PartitionSpec as P

SIDE = 32
LAYERS = 3
ROUNDS = 2
SPAN = 2 * ROUNDS + 1
LANES = 128
ROWS = 8
BIAS = 0.1
BELOW_ONE = 1.0 - 2.0**-24
MESH = pl.DeviceIdType.MESH

ARC = (
    0.3183098449892848,
    -0.02253203775558662,
    0.005946535585369838,
    -0.002275705294168609,
    0.0008254564785290766,
    -0.00016869743862866002,
)


def stencil_sum(groups, masks):
    first, last, not_left, not_right = masks
    tall = []
    for maps in groups:
        above = jnp.where(first, 0.0, pltpu.roll(maps[-1], SIDE, 1))
        below = jnp.where(last, 0.0, pltpu.roll(maps[0], LANES - SIDE, 1))
        column = [above] + list(maps) + [below]
        pairs = [x + y for x, y in zip(column[:-1], column[1:])]
        tall.append([pairs[k] + column[k + 2] for k in range(len(maps))])
    out = []
    for maps in tall:
        left = [jnp.where(not_left, pltpu.roll(x, 1, 1), 0.0) for x in maps]
        right = [jnp.where(not_right, pltpu.roll(x, LANES - 1, 1), 0.0) for x in maps]
        out.append([x + (y + z) for x, y, z in zip(maps, left, right)])
    return out


def lane_masks():
    lane = lax.broadcasted_iota(jnp.int32, (ROWS, LANES), 1)
    col = lane % SIDE
    return lane < SIDE, lane >= LANES - SIDE, col != 0, col != SIDE - 1


def channel_sum(terms):
    total = terms[0]
    for term in terms[1:]:
        total = total + term
    return total


def affine(groups, factor):
    return [[x * factor + BIAS for x in maps] for maps in groups]


def roots_of(maps):
    inverse = [lax.rsqrt(x) for x in maps]
    return [x * y for x, y in zip(maps, inverse)], inverse


def twice_relu(cov, scale, inverse):
    a = jnp.minimum(jnp.abs(cov) * inverse, BELOW_ONE)
    y = 1.0 - a
    poly = ARC[-1]
    for c in ARC[-2::-1]:
        poly = poly * a + c
    bent = y * y * lax.rsqrt(y) * poly
    return scale * bent + jnp.minimum(jnp.maximum(cov, 0.0), scale)


def kernel(
    n_blk, n_grp, images, out, raw, turn, got, own, flat, root, inv, wide, res,
    raw_sem, send, recv,
):
    b, z = lax.axis_index("blk"), lax.axis_index("grp")
    chan, per, pix = images.shape
    chunks = pix // LANES
    image_rows = chan * chunks
    block = per * n_grp
    units = block // ROWS
    sources = ROWS // per
    offsets = [d for d in range(-ROUNDS, ROUNDS + 1) if d]

    load = pltpu.make_async_copy(images, raw, raw_sem)
    load.start()
    barrier = pltpu.get_barrier_semaphore()
    def source_of(order):
        if isinstance(order, int) and order == 0:
            return z
        mate = z + 1 - 2 * lax.rem(z, 2)
        far = lax.rem(z // 2 * 2 + order, n_grp)
        if isinstance(order, int):
            return mate if order == 1 else far
        return jnp.where(order == 0, z, jnp.where(order == 1, mate, far))

    partners = [(0, d) for d in offsets] + [(1, d) for d in [0] + offsets]
    partners += [(order, 0) for order in range(2, n_grp)]
    partners = [
        (order, d, {"blk": lax.rem(b + d + n_blk, n_blk), "grp": source_of(order)})
        for order, d in partners
    ]
    for order, d, device in partners:
        pl.semaphore_signal(barrier, inc=1, device_id=device, device_id_type=MESH)
    load.wait()

    data = raw[...].astype(jnp.float32)
    for k in range(chunks):
        for c in range(chan):
            turn[pl.ds(k * ROWS + c, per, stride=chan), :] = data[
                c, :, k * LANES : (k + 1) * LANES
            ]
    lane = lax.broadcasted_iota(jnp.int32, (ROWS, LANES), 1)
    natural = [turn[k * ROWS : (k + 1) * ROWS, :] for k in range(chunks)]
    fold = LANES // SIDE
    for k in range(chunks):
        row = None
        for g in range(fold):
            at = g * chunks + k
            part = natural[at // fold]
            shift = (g - at % fold) * SIDE % LANES
            part = pltpu.roll(part, shift, 1) if shift else part
            row = part if row is None else jnp.where(lane >= g * SIDE, part, row)
        flat[pl.ds(k, per * chan, stride=chunks), :] = row[: per * chan]
    got[ROUNDS, z] = flat[...].astype(jnp.bfloat16)

    pl.semaphore_wait(barrier, len(partners))

    copies = []

    def give(order, source, d, device):
        copy = pltpu.make_async_remote_copy(
            src_ref=got.at[ROUNDS, source],
            dst_ref=got.at[ROUNDS - d, source],
            send_sem=send.at[order, ROUNDS + d],
            recv_sem=recv.at[ROUNDS - d, source],
            device_id=device,
            device_id_type=MESH,
        )
        copy.start()
        copies.append(copy)

    for order, d, device in sorted(partners, key=lambda p: p[0] < 2):
        give(order, z, d, device)

    masks = lane_masks()
    current = []
    for i in range(per):
        squares = []
        for k in range(chunks):
            parts = []
            for c in range(chan):
                row = i * image_rows + c * chunks + k
                part = jnp.broadcast_to(flat[row : row + 1, :], (ROWS, LANES))
                own[row] = part
                parts.append(part * part)
            squares.append(channel_sum(parts))
        current.append(squares)
    for layer in range(LAYERS):
        factor = 1.0 / 9 if layer else 1.0 / (9 * chan)
        current = affine(stencil_sum(current, masks), factor)
        for i in range(per):
            roots, inverses = roots_of(current[i])
            for k in range(chunks):
                at = (i * LAYERS + layer) * chunks + k
                root[at] = roots[k]
                inv[at] = inverses[k]

    def arrived(k, source):
        pltpu.make_async_remote_copy(
            src_ref=got.at[k, source],
            dst_ref=got.at[k, source],
            send_sem=send.at[0, ROUNDS],
            recv_sem=recv.at[k, source],
            device_id={"grp": z},
            device_id_type=MESH,
        ).wait_recv()

    for order in range(2, n_grp):
        source = source_of(order)
        arrived(ROUNDS, source)
        for d in offsets:
            give(order, source, d, {"blk": lax.rem(b + d + n_blk, n_blk)})
    arrived(ROUNDS, source_of(1))

    def work(members):
        maps = []
        for m, (places, slot) in enumerate(members):
            for s, (k, source) in enumerate(places):
                wide[m, s * per * image_rows : (s + 1) * per * image_rows, :] = got[
                    k, source
                ].astype(jnp.float32)
            theirs = [
                [wide[m, pl.ds(c * chunks + j, ROWS, stride=image_rows), :] for c in range(chan)]
                for j in range(chunks)
            ]
            maps.append([channel_sum([x * x for x in parts]) for parts in theirs])
            for i in range(per):
                maps.append(
                    [
                        channel_sum(
                            [
                                own[i * image_rows + c * chunks + j] * theirs[j][c]
                                for c in range(chan)
                            ]
                        )
                        for j in range(chunks)
                    ]
                )
        for layer in range(LAYERS):
            factor = 1.0 / 9 if layer else 1.0 / (9 * chan)
            maps = affine(stencil_sum(maps, masks), factor)
            for m in range(len(members)):
                roots, inverses = roots_of(maps[m * (per + 1)])
                for i in range(per):
                    at = (i * LAYERS + layer) * chunks
                    cov = maps[m * (per + 1) + 1 + i]
                    maps[m * (per + 1) + 1 + i] = [
                        twice_relu(cov[j], root[at + j] * roots[j], inv[at + j] * inverses[j])
                        for j in range(chunks)
                    ]
        for m, (places, slot) in enumerate(members):
            for i in range(per):
                res[i, slot] = channel_sum(maps[m * (per + 1) + 1 + i])

    def member(t):
        home = jnp.int32((t >= 1) & (t <= units))
        away = 1 - home
        order = jnp.where(t > units, t - units, 0)
        source = source_of(order)

        @pl.when(home == 0)
        def _():
            for d in offsets:
                arrived(ROUNDS + d, source)

        unit = home * (t - 1)
        places = [
            (ROUNDS + away * d, away * source + home * (unit * sources + s))
            for s, d in enumerate(offsets)
        ]
        return places, home * unit + away * (units + source)

    total_units = units + n_grp

    def step(t, carry):
        work([member(2 * t), member(2 * t + 1)])
        return carry

    lax.fori_loop(0, total_units // 2, step, 0)
    if total_units % 2:
        work([member(jnp.int32(total_units - 1))])

    row = lax.broadcasted_iota(jnp.int32, (ROWS, LANES), 0)
    lane = lax.broadcasted_iota(jnp.int32, (ROWS, LANES), 1)
    for i in range(per):
        sums = [
            jnp.sum(res[i, slot], axis=1, keepdims=True) * (1.0 / pix)
            for slot in range(units + n_grp)
        ]
        home = jnp.zeros((ROWS, LANES), jnp.float32)
        for unit in range(units):
            home = jnp.where(lane == row + unit * ROWS, sums[unit], home)
        out[ROUNDS, i : i + 1, :] = jnp.sum(home, axis=0, keepdims=True)[:, :block]
        away = jnp.zeros((ROWS, LANES), jnp.float32)
        for source in range(n_grp):
            mine = (lane // per == source) & (lane % per == row % per)
            away = jnp.where(mine, sums[units + source], away)
        total = away
        for r in range(1, per):
            total = total + pltpu.roll(away, ROWS - r, 0)
        for at, d in enumerate(offsets):
            out[ROUNDS + d, i : i + 1, :] = total[at * per : at * per + 1, :block]
    for copy in copies:
        copy.wait_send()


def per_device(n_blk, n_grp, images):
    per, chan, pix = images.shape
    chunks = pix // LANES
    rows = per * chan * chunks
    block = per * n_grp
    assert n_grp % 2 == 0 and block % ROWS == 0 and per * (SPAN - 1) == ROWS
    maps = per * LAYERS * chunks
    window = pl.pallas_call(
        functools.partial(kernel, n_blk, n_grp),
        out_shape=jax.ShapeDtypeStruct((SPAN, per, block), jnp.float32),
        in_specs=[pl.BlockSpec(memory_space=pltpu.HBM)],
        out_specs=pl.BlockSpec(memory_space=pltpu.VMEM),
        scratch_shapes=[
            pltpu.VMEM((chan, per, pix), jnp.bfloat16),
            pltpu.VMEM((chunks * ROWS, LANES), jnp.float32),
            pltpu.VMEM((SPAN, n_grp, rows, LANES), jnp.bfloat16),
            pltpu.VMEM((rows, ROWS, LANES), jnp.float32),
            pltpu.VMEM((rows, LANES), jnp.float32),
            pltpu.VMEM((maps, ROWS, LANES), jnp.float32),
            pltpu.VMEM((maps, ROWS, LANES), jnp.float32),
            pltpu.VMEM((2, ROWS * chan * chunks, LANES), jnp.float32),
            pltpu.VMEM((per, block // ROWS + n_grp, ROWS, LANES), jnp.float32),
            pltpu.SemaphoreType.DMA,
            pltpu.SemaphoreType.DMA((n_grp, SPAN)),
            pltpu.SemaphoreType.DMA((SPAN, n_grp)),
        ],
        compiler_params=pltpu.CompilerParams(
            collective_id=0, has_side_effects=True, vmem_limit_bytes=32 * 1024 * 1024
        ),
    )(jnp.transpose(images, (1, 0, 2)))
    return jnp.transpose(window, (1, 0, 2))


def solution(mesh):
    spec = P(("blk", "grp"), None, None)
    body = functools.partial(per_device, mesh.shape["blk"], mesh.shape["grp"])
    return jax.shard_map(body, mesh=mesh, in_specs=(spec,), out_specs=spec, check_vma=False)
```

```python
import functools

import jax
import jax.numpy as jnp
from jax import lax
from jax.experimental import pallas as pl
from jax.experimental.pallas import tpu as pltpu
from jax.sharding import PartitionSpec as P

SIDE = 32
LAYERS = 3
ROUNDS = 2
SPAN = 2 * ROUNDS + 1
LANES = 128
ROWS = 8
BIAS = 0.1
BELOW_ONE = 1.0 - 2.0**-24
MESH = pl.DeviceIdType.MESH

ARC = (
    0.3183098449892848,
    -0.02253203775558662,
    0.005946535585369838,
    -0.002275705294168609,
    0.0008254564785290766,
    -0.00016869743862866002,
)


def stencil_sum(groups, masks):
    first, last, not_left, not_right = masks
    tall = []
    for maps in groups:
        above = jnp.where(first, 0.0, pltpu.roll(maps[-1], SIDE, 1))
        below = jnp.where(last, 0.0, pltpu.roll(maps[0], LANES - SIDE, 1))
        column = [above] + list(maps) + [below]
        pairs = [x + y for x, y in zip(column[:-1], column[1:])]
        tall.append([pairs[k] + column[k + 2] for k in range(len(maps))])
    out = []
    for maps in tall:
        left = [jnp.where(not_left, pltpu.roll(x, 1, 1), 0.0) for x in maps]
        right = [jnp.where(not_right, pltpu.roll(x, LANES - 1, 1), 0.0) for x in maps]
        out.append([x + (y + z) for x, y, z in zip(maps, left, right)])
    return out


def lane_masks():
    lane = lax.broadcasted_iota(jnp.int32, (ROWS, LANES), 1)
    col = lane % SIDE
    return lane < SIDE, lane >= LANES - SIDE, col != 0, col != SIDE - 1


def channel_sum(terms):
    total = terms[0]
    for term in terms[1:]:
        total = total + term
    return total


def affine(groups, factor):
    return [[x * factor + BIAS for x in maps] for maps in groups]


def roots_of(maps):
    inverse = [lax.rsqrt(x) for x in maps]
    return [x * y for x, y in zip(maps, inverse)], inverse


def twice_relu(cov, scale, inverse):
    a = jnp.minimum(jnp.abs(cov) * inverse, BELOW_ONE)
    y = 1.0 - a
    poly = ARC[-1]
    for c in ARC[-2::-1]:
        poly = poly * a + c
    bent = y * y * lax.rsqrt(y) * poly
    return scale * bent + jnp.minimum(jnp.maximum(cov, 0.0), scale)


def kernel(
    n_blk, n_grp, images, out, turn, got, own, flat, root, inv, wide, res,
    grp_send, grp_recv, blk_send, blk_recv,
):
    b, z = lax.axis_index("blk"), lax.axis_index("grp")
    chan, per, pix = images.shape
    chunks = pix // LANES
    image_rows = chan * chunks
    block = per * n_grp
    units = block // ROWS
    sources = ROWS // per
    offsets = [d for d in range(-ROUNDS, ROUNDS + 1) if d]

    barrier = pltpu.get_barrier_semaphore()
    for dz in range(1, n_grp):
        pl.semaphore_signal(
            barrier, inc=1, device_id={"grp": lax.rem(z + dz, n_grp)}, device_id_type=MESH
        )
    for d in offsets:
        pl.semaphore_signal(
            barrier, inc=1, device_id={"blk": lax.rem(b + d + n_blk, n_blk)}, device_id_type=MESH
        )

    data = images[...].astype(jnp.float32)
    for k in range(chunks):
        for c in range(chan):
            turn[pl.ds(k * ROWS + c, per, stride=chan), :] = data[
                c, :, k * LANES : (k + 1) * LANES
            ]
    lane = lax.broadcasted_iota(jnp.int32, (ROWS, LANES), 1)
    natural = [turn[k * ROWS : (k + 1) * ROWS, :] for k in range(chunks)]
    fold = LANES // SIDE
    for k in range(chunks):
        row = None
        for g in range(fold):
            at = g * chunks + k
            part = natural[at // fold]
            shift = (g - at % fold) * SIDE % LANES
            part = pltpu.roll(part, shift, 1) if shift else part
            row = part if row is None else jnp.where(lane >= g * SIDE, part, row)
        flat[pl.ds(k, per * chan, stride=chunks), :] = row[: per * chan]
    got[ROUNDS, 0] = flat[...].astype(jnp.bfloat16)

    pl.semaphore_wait(barrier, n_grp - 1 + len(offsets))

    copies = []
    for dz in range(1, n_grp):
        copy = pltpu.make_async_remote_copy(
            src_ref=got.at[ROUNDS, 0],
            dst_ref=got.at[ROUNDS, n_grp - dz],
            send_sem=grp_send.at[dz],
            recv_sem=grp_recv.at[n_grp - dz],
            device_id={"grp": lax.rem(z + dz, n_grp)},
            device_id_type=MESH,
        )
        copy.start()
        copies.append(copy)

    stages = [pl.ds(0, 1), pl.ds(1, n_grp - 1)]

    def pass_on(stage):
        for at, d in enumerate(offsets):
            copy = pltpu.make_async_remote_copy(
                src_ref=got.at[ROUNDS, stages[stage]],
                dst_ref=got.at[ROUNDS + d, stages[stage]],
                send_sem=blk_send.at[stage, at],
                recv_sem=blk_recv.at[stage, at],
                device_id={"blk": lax.rem(b - d + n_blk, n_blk)},
                device_id_type=MESH,
            )
            copy.start()
            copies.append(copy)

    pass_on(0)

    masks = lane_masks()
    current = []
    for i in range(per):
        squares = []
        for k in range(chunks):
            parts = []
            for c in range(chan):
                row = i * image_rows + c * chunks + k
                part = jnp.broadcast_to(flat[row : row + 1, :], (ROWS, LANES))
                own[row] = part
                parts.append(part * part)
            squares.append(channel_sum(parts))
        current.append(squares)
    for layer in range(LAYERS):
        factor = 1.0 / 9 if layer else 1.0 / (9 * chan)
        current = affine(stencil_sum(current, masks), factor)
        for i in range(per):
            roots, inverses = roots_of(current[i])
            for k in range(chunks):
                at = (i * LAYERS + layer) * chunks + k
                root[at] = roots[k]
                inv[at] = inverses[k]

    def arrived(ref, sem):
        pltpu.make_async_remote_copy(
            src_ref=ref,
            dst_ref=ref,
            send_sem=grp_send.at[0],
            recv_sem=sem,
            device_id={"grp": z},
            device_id_type=MESH,
        ).wait_recv()

    for dz in range(1, n_grp):
        arrived(got.at[ROUNDS, dz], grp_recv.at[dz])
    pass_on(1)

    def work(members):
        maps = []
        for m, (places, slot) in enumerate(members):
            for s, (k, source) in enumerate(places):
                wide[m, s * per * image_rows : (s + 1) * per * image_rows, :] = got[
                    k, source
                ].astype(jnp.float32)
            theirs = [
                [wide[m, pl.ds(c * chunks + j, ROWS, stride=image_rows), :] for c in range(chan)]
                for j in range(chunks)
            ]
            maps.append([channel_sum([x * x for x in parts]) for parts in theirs])
            for i in range(per):
                maps.append(
                    [
                        channel_sum(
                            [
                                own[i * image_rows + c * chunks + j] * theirs[j][c]
                                for c in range(chan)
                            ]
                        )
                        for j in range(chunks)
                    ]
                )
        for layer in range(LAYERS):
            factor = 1.0 / 9 if layer else 1.0 / (9 * chan)
            maps = affine(stencil_sum(maps, masks), factor)
            for m in range(len(members)):
                roots, inverses = roots_of(maps[m * (per + 1)])
                for i in range(per):
                    at = (i * LAYERS + layer) * chunks
                    cov = maps[m * (per + 1) + 1 + i]
                    maps[m * (per + 1) + 1 + i] = [
                        twice_relu(cov[j], root[at + j] * roots[j], inv[at + j] * inverses[j])
                        for j in range(chunks)
                    ]
        for m, (places, slot) in enumerate(members):
            for i in range(per):
                res[i, slot] = channel_sum(maps[m * (per + 1) + 1 + i])

    def member(t):
        home = jnp.int32((t >= 1) & (t <= units))
        away = 1 - home
        order = jnp.where(t > units, t - units, 0)
        source = lax.rem(z + order, n_grp)

        for stage, when in enumerate((0, units + 1)):

            @pl.when(t == when)
            def _():
                for at, d in enumerate(offsets):
                    arrived(got.at[ROUNDS + d, stages[stage]], blk_recv.at[stage, at])

        unit = home * (t - 1)
        places = [
            (
                ROUNDS + away * d,
                away * order + home * lax.rem(unit * sources + s - z + n_grp, n_grp),
            )
            for s, d in enumerate(offsets)
        ]
        return places, home * unit + away * (units + source)

    total_units = units + n_grp

    def step(t, carry):
        work([member(2 * t), member(2 * t + 1)])
        return carry

    lax.fori_loop(0, total_units // 2, step, 0)
    if total_units % 2:
        work([member(jnp.int32(total_units - 1))])

    row = lax.broadcasted_iota(jnp.int32, (ROWS, LANES), 0)
    lane = lax.broadcasted_iota(jnp.int32, (ROWS, LANES), 1)
    for i in range(per):
        sums = [
            jnp.sum(res[i, slot], axis=1, keepdims=True) * (1.0 / pix)
            for slot in range(units + n_grp)
        ]
        home = jnp.zeros((ROWS, LANES), jnp.float32)
        for unit in range(units):
            home = jnp.where(lane == row + unit * ROWS, sums[unit], home)
        out[ROUNDS, i : i + 1, :] = jnp.sum(home, axis=0, keepdims=True)[:, :block]
        away = jnp.zeros((ROWS, LANES), jnp.float32)
        for source in range(n_grp):
            mine = (lane // per == source) & (lane % per == row % per)
            away = jnp.where(mine, sums[units + source], away)
        total = away
        for r in range(1, per):
            total = total + pltpu.roll(away, ROWS - r, 0)
        for at, d in enumerate(offsets):
            out[ROUNDS + d, i : i + 1, :] = total[at * per : at * per + 1, :block]
    for copy in copies:
        copy.wait_send()


def per_device(n_blk, n_grp, images):
    per, chan, pix = images.shape
    chunks = pix // LANES
    rows = per * chan * chunks
    block = per * n_grp
    assert block % ROWS == 0 and per * (SPAN - 1) == ROWS
    maps = per * LAYERS * chunks
    window = pl.pallas_call(
        functools.partial(kernel, n_blk, n_grp),
        out_shape=jax.ShapeDtypeStruct((SPAN, per, block), jnp.float32),
        in_specs=[pl.BlockSpec(memory_space=pltpu.VMEM)],
        out_specs=pl.BlockSpec(memory_space=pltpu.VMEM),
        scratch_shapes=[
            pltpu.VMEM((chunks * ROWS, LANES), jnp.float32),
            pltpu.VMEM((SPAN, n_grp, rows, LANES), jnp.bfloat16),
            pltpu.VMEM((rows, ROWS, LANES), jnp.float32),
            pltpu.VMEM((rows, LANES), jnp.float32),
            pltpu.VMEM((maps, ROWS, LANES), jnp.float32),
            pltpu.VMEM((maps, ROWS, LANES), jnp.float32),
            pltpu.VMEM((2, ROWS * chan * chunks, LANES), jnp.float32),
            pltpu.VMEM((per, block // ROWS + n_grp, ROWS, LANES), jnp.float32),
            pltpu.SemaphoreType.DMA((n_grp,)),
            pltpu.SemaphoreType.DMA((n_grp,)),
            pltpu.SemaphoreType.DMA((2, SPAN - 1)),
            pltpu.SemaphoreType.DMA((2, SPAN - 1)),
        ],
        compiler_params=pltpu.CompilerParams(
            collective_id=0, has_side_effects=True, vmem_limit_bytes=32 * 1024 * 1024
        ),
    )(jnp.transpose(images, (1, 0, 2)))
    return jnp.transpose(window, (1, 0, 2))


def solution(mesh):
    spec = P(("blk", "grp"), None, None)
    body = functools.partial(per_device, mesh.shape["blk"], mesh.shape["grp"])
    return jax.shard_map(body, mesh=mesh, in_specs=(spec,), out_specs=spec, check_vma=False)
```

```python
import functools

import jax
import jax.numpy as jnp
from jax import lax
from jax.experimental import pallas as pl
from jax.experimental.pallas import tpu as pltpu
from jax.sharding import PartitionSpec as P

SIDE = 32
LAYERS = 3
ROUNDS = 2
SPAN = 2 * ROUNDS + 1
LANES = 128
ROWS = 8
BIAS = 0.1
BELOW_ONE = 1.0 - 2.0**-24
MESH = pl.DeviceIdType.MESH

ARC = (
    0.3183098449892848,
    -0.02253203775558662,
    0.005946535585369838,
    -0.002275705294168609,
    0.0008254564785290766,
    -0.00016869743862866002,
)


def stencil_sum(groups, masks):
    first, last, not_left, not_right = masks
    tall = []
    for maps in groups:
        above = jnp.where(first, 0.0, pltpu.roll(maps[-1], SIDE, 1))
        below = jnp.where(last, 0.0, pltpu.roll(maps[0], LANES - SIDE, 1))
        column = [above] + list(maps) + [below]
        pairs = [x + y for x, y in zip(column[:-1], column[1:])]
        tall.append([pairs[k] + column[k + 2] for k in range(len(maps))])
    out = []
    for maps in tall:
        left = [jnp.where(not_left, pltpu.roll(x, 1, 1), 0.0) for x in maps]
        right = [jnp.where(not_right, pltpu.roll(x, LANES - 1, 1), 0.0) for x in maps]
        out.append([x + (y + z) for x, y, z in zip(maps, left, right)])
    return out


def lane_masks():
    lane = lax.broadcasted_iota(jnp.int32, (ROWS, LANES), 1)
    col = lane % SIDE
    return lane < SIDE, lane >= LANES - SIDE, col != 0, col != SIDE - 1


def channel_sum(terms):
    total = terms[0]
    for term in terms[1:]:
        total = total + term
    return total


def affine(groups, factor):
    return [[x * factor + BIAS for x in maps] for maps in groups]


def roots_of(maps):
    inverse = [lax.rsqrt(x) for x in maps]
    return [x * y for x, y in zip(maps, inverse)], inverse


def twice_relu(cov, scale, inverse):
    a = jnp.minimum(jnp.abs(cov) * inverse, BELOW_ONE)
    y = 1.0 - a
    poly = ARC[-1]
    for c in ARC[-2::-1]:
        poly = poly * a + c
    bent = y * y * lax.rsqrt(y) * poly
    return scale * bent + jnp.minimum(jnp.maximum(cov, 0.0), scale)


def kernel(
    n_blk, n_grp, images, out, turn, got, own, flat, root, inv, wide, res,
    send, recv,
):
    b, z = lax.axis_index("blk"), lax.axis_index("grp")
    chan, per, pix = images.shape
    chunks = pix // LANES
    image_rows = chan * chunks
    block = per * n_grp
    units = block // ROWS
    sources = ROWS // per
    offsets = [d for d in range(-ROUNDS, ROUNDS + 1) if d]

    barrier = pltpu.get_barrier_semaphore()
    def source_of(order):
        if isinstance(order, int) and order == 0:
            return z
        mate = z + 1 - 2 * lax.rem(z, 2)
        far = lax.rem(z // 2 * 2 + order, n_grp)
        if isinstance(order, int):
            return mate if order == 1 else far
        return jnp.where(order == 0, z, jnp.where(order == 1, mate, far))

    partners = [(0, d) for d in offsets] + [(1, d) for d in [0] + offsets]
    partners += [(order, 0) for order in range(2, n_grp)]
    partners = [
        (order, d, {"blk": lax.rem(b + d + n_blk, n_blk), "grp": source_of(order)})
        for order, d in partners
    ]
    for order, d, device in partners:
        pl.semaphore_signal(barrier, inc=1, device_id=device, device_id_type=MESH)

    data = images[...].astype(jnp.float32)
    for k in range(chunks):
        for c in range(chan):
            turn[pl.ds(k * ROWS + c, per, stride=chan), :] = data[
                c, :, k * LANES : (k + 1) * LANES
            ]
    lane = lax.broadcasted_iota(jnp.int32, (ROWS, LANES), 1)
    natural = [turn[k * ROWS : (k + 1) * ROWS, :] for k in range(chunks)]
    fold = LANES // SIDE
    for k in range(chunks):
        row = None
        for g in range(fold):
            at = g * chunks + k
            part = natural[at // fold]
            shift = (g - at % fold) * SIDE % LANES
            part = pltpu.roll(part, shift, 1) if shift else part
            row = part if row is None else jnp.where(lane >= g * SIDE, part, row)
        flat[pl.ds(k, per * chan, stride=chunks), :] = row[: per * chan]
    got[ROUNDS, z] = flat[...].astype(jnp.bfloat16)

    pl.semaphore_wait(barrier, len(partners))

    copies = []

    def give(order, source, d, device):
        copy = pltpu.make_async_remote_copy(
            src_ref=got.at[ROUNDS, source],
            dst_ref=got.at[ROUNDS - d, source],
            send_sem=send.at[order, ROUNDS + d],
            recv_sem=recv.at[ROUNDS - d, source],
            device_id=device,
            device_id_type=MESH,
        )
        copy.start()
        copies.append(copy)

    for order, d, device in sorted(partners, key=lambda p: p[0] < 2):
        give(order, z, d, device)

    masks = lane_masks()
    current = []
    for i in range(per):
        squares = []
        for k in range(chunks):
            parts = []
            for c in range(chan):
                row = i * image_rows + c * chunks + k
                part = jnp.broadcast_to(flat[row : row + 1, :], (ROWS, LANES))
                own[row] = part
                parts.append(part * part)
            squares.append(channel_sum(parts))
        current.append(squares)
    for layer in range(LAYERS):
        factor = 1.0 / 9 if layer else 1.0 / (9 * chan)
        current = affine(stencil_sum(current, masks), factor)
        for i in range(per):
            roots, inverses = roots_of(current[i])
            for k in range(chunks):
                at = (i * LAYERS + layer) * chunks + k
                root[at] = roots[k]
                inv[at] = inverses[k]

    def arrived(k, source):
        pltpu.make_async_remote_copy(
            src_ref=got.at[k, source],
            dst_ref=got.at[k, source],
            send_sem=send.at[0, ROUNDS],
            recv_sem=recv.at[k, source],
            device_id={"grp": z},
            device_id_type=MESH,
        ).wait_recv()

    for order in range(2, n_grp):
        source = source_of(order)
        arrived(ROUNDS, source)
        for d in offsets:
            give(order, source, d, {"blk": lax.rem(b + d + n_blk, n_blk)})
    arrived(ROUNDS, source_of(1))

    def work(members):
        maps = []
        for m, (places, slot) in enumerate(members):
            for s, (k, source) in enumerate(places):
                wide[m, s * per * image_rows : (s + 1) * per * image_rows, :] = got[
                    k, source
                ].astype(jnp.float32)
            theirs = [
                [wide[m, pl.ds(c * chunks + j, ROWS, stride=image_rows), :] for c in range(chan)]
                for j in range(chunks)
            ]
            maps.append([channel_sum([x * x for x in parts]) for parts in theirs])
            for i in range(per):
                maps.append(
                    [
                        channel_sum(
                            [
                                own[i * image_rows + c * chunks + j] * theirs[j][c]
                                for c in range(chan)
                            ]
                        )
                        for j in range(chunks)
                    ]
                )
        for layer in range(LAYERS):
            factor = 1.0 / 9 if layer else 1.0 / (9 * chan)
            maps = affine(stencil_sum(maps, masks), factor)
            for m in range(len(members)):
                roots, inverses = roots_of(maps[m * (per + 1)])
                for i in range(per):
                    at = (i * LAYERS + layer) * chunks
                    cov = maps[m * (per + 1) + 1 + i]
                    maps[m * (per + 1) + 1 + i] = [
                        twice_relu(cov[j], root[at + j] * roots[j], inv[at + j] * inverses[j])
                        for j in range(chunks)
                    ]
        for m, (places, slot) in enumerate(members):
            for i in range(per):
                res[i, slot] = channel_sum(maps[m * (per + 1) + 1 + i])

    def member(t):
        home = jnp.int32((t >= 1) & (t <= units))
        away = 1 - home
        order = jnp.where(t > units, t - units, 0)
        source = source_of(order)

        @pl.when(home == 0)
        def _():
            for d in offsets:
                arrived(ROUNDS + d, source)

        unit = home * (t - 1)
        places = [
            (ROUNDS + away * d, away * source + home * (unit * sources + s))
            for s, d in enumerate(offsets)
        ]
        return places, home * unit + away * (units + source)

    total_units = units + n_grp

    def step(t, carry):
        work([member(t)])
        return carry

    lax.fori_loop(0, total_units, step, 0)

    row = lax.broadcasted_iota(jnp.int32, (ROWS, LANES), 0)
    lane = lax.broadcasted_iota(jnp.int32, (ROWS, LANES), 1)
    for i in range(per):
        sums = [
            jnp.sum(res[i, slot], axis=1, keepdims=True) * (1.0 / pix)
            for slot in range(units + n_grp)
        ]
        home = jnp.zeros((ROWS, LANES), jnp.float32)
        for unit in range(units):
            home = jnp.where(lane == row + unit * ROWS, sums[unit], home)
        out[ROUNDS, i : i + 1, :] = jnp.sum(home, axis=0, keepdims=True)[:, :block]
        away = jnp.zeros((ROWS, LANES), jnp.float32)
        for source in range(n_grp):
            mine = (lane // per == source) & (lane % per == row % per)
            away = jnp.where(mine, sums[units + source], away)
        total = away
        for r in range(1, per):
            total = total + pltpu.roll(away, ROWS - r, 0)
        for at, d in enumerate(offsets):
            out[ROUNDS + d, i : i + 1, :] = total[at * per : at * per + 1, :block]
    for copy in copies:
        copy.wait_send()


def per_device(n_blk, n_grp, images):
    per, chan, pix = images.shape
    chunks = pix // LANES
    rows = per * chan * chunks
    block = per * n_grp
    assert n_grp % 2 == 0 and block % ROWS == 0 and per * (SPAN - 1) == ROWS
    maps = per * LAYERS * chunks
    window = pl.pallas_call(
        functools.partial(kernel, n_blk, n_grp),
        out_shape=jax.ShapeDtypeStruct((SPAN, per, block), jnp.float32),
        in_specs=[pl.BlockSpec(memory_space=pltpu.VMEM)],
        out_specs=pl.BlockSpec(memory_space=pltpu.VMEM),
        scratch_shapes=[
            pltpu.VMEM((chunks * ROWS, LANES), jnp.float32),
            pltpu.VMEM((SPAN, n_grp, rows, LANES), jnp.bfloat16),
            pltpu.VMEM((rows, ROWS, LANES), jnp.float32),
            pltpu.VMEM((rows, LANES), jnp.float32),
            pltpu.VMEM((maps, ROWS, LANES), jnp.float32),
            pltpu.VMEM((maps, ROWS, LANES), jnp.float32),
            pltpu.VMEM((1, ROWS * chan * chunks, LANES), jnp.float32),
            pltpu.VMEM((per, block // ROWS + n_grp, ROWS, LANES), jnp.float32),
            pltpu.SemaphoreType.DMA((n_grp, SPAN)),
            pltpu.SemaphoreType.DMA((SPAN, n_grp)),
        ],
        compiler_params=pltpu.CompilerParams(
            collective_id=0, has_side_effects=True, vmem_limit_bytes=32 * 1024 * 1024
        ),
    )(jnp.transpose(images, (1, 0, 2)))
    return jnp.transpose(window, (1, 0, 2))


def solution(mesh):
    spec = P(("blk", "grp"), None, None)
    body = functools.partial(per_device, mesh.shape["blk"], mesh.shape["grp"])
    return jax.shard_map(body, mesh=mesh, in_specs=(spec,), out_specs=spec, check_vma=False)
```

```python
import functools

import jax
import jax.numpy as jnp
from jax import lax
from jax.experimental import pallas as pl
from jax.experimental.pallas import tpu as pltpu
from jax.sharding import PartitionSpec as P

SIDE = 32
LAYERS = 3
ROUNDS = 2
SPAN = 2 * ROUNDS + 1
LANES = 128
ROWS = 8
BIAS = 0.1
BELOW_ONE = 1.0 - 2.0**-24
MESH = pl.DeviceIdType.MESH

ARC = (
    0.3183095237082206,
    -0.02251588221055572,
    0.005816643278465437,
    -0.0019102241839555419,
    0.00040573672732109817,
)


def stencil_sum(groups, masks):
    first, last, not_left, not_right = masks
    tall = []
    for maps in groups:
        above = jnp.where(first, 0.0, pltpu.roll(maps[-1], SIDE, 1))
        below = jnp.where(last, 0.0, pltpu.roll(maps[0], LANES - SIDE, 1))
        column = [above] + list(maps) + [below]
        pairs = [x + y for x, y in zip(column[:-1], column[1:])]
        tall.append([pairs[k] + column[k + 2] for k in range(len(maps))])
    out = []
    for maps in tall:
        left = [jnp.where(not_left, pltpu.roll(x, 1, 1), 0.0) for x in maps]
        right = [jnp.where(not_right, pltpu.roll(x, LANES - 1, 1), 0.0) for x in maps]
        out.append([x + (y + z) for x, y, z in zip(maps, left, right)])
    return out


def lane_masks():
    lane = lax.broadcasted_iota(jnp.int32, (ROWS, LANES), 1)
    col = lane % SIDE
    return lane < SIDE, lane >= LANES - SIDE, col != 0, col != SIDE - 1


def channel_sum(terms):
    total = terms[0]
    for term in terms[1:]:
        total = total + term
    return total


def map_scale(channels, layer):
    return float(channels * 9 ** (layer + 1))


def biased(groups, scale):
    return [[x + BIAS * scale for x in maps] for maps in groups]


def roots_of(maps):
    inverse = [lax.rsqrt(x) for x in maps]
    return [x * y for x, y in zip(maps, inverse)], inverse


def twice_relu(cov, scale, inverse):
    a = jnp.minimum(jnp.abs(cov) * inverse, BELOW_ONE)
    y = 1.0 - a
    poly = ARC[-1]
    for c in ARC[-2::-1]:
        poly = poly * a + c
    bent = y * y * lax.rsqrt(y) * poly
    return scale * bent + jnp.minimum(jnp.maximum(cov, 0.0), scale)


def kernel(
    n_blk, n_grp, images, out, turn, got, own, flat, root, inv, wide, res,
    send, recv,
):
    b, z = lax.axis_index("blk"), lax.axis_index("grp")
    chan, per, pix = images.shape
    chunks = pix // LANES
    image_rows = chan * chunks
    block = per * n_grp
    units = block // ROWS
    sources = ROWS // per
    offsets = [d for d in range(-ROUNDS, ROUNDS + 1) if d]

    barrier = pltpu.get_barrier_semaphore()
    def source_of(order):
        if isinstance(order, int) and order == 0:
            return z
        mate = z + 1 - 2 * lax.rem(z, 2)
        far = lax.rem(z // 2 * 2 + order, n_grp)
        if isinstance(order, int):
            return mate if order == 1 else far
        return jnp.where(order == 0, z, jnp.where(order == 1, mate, far))

    partners = [(0, d) for d in offsets] + [(1, d) for d in [0] + offsets]
    partners += [(order, 0) for order in range(2, n_grp)]
    partners = [
        (order, d, {"blk": lax.rem(b + d + n_blk, n_blk), "grp": source_of(order)})
        for order, d in partners
    ]
    for order, d, device in partners:
        pl.semaphore_signal(barrier, inc=1, device_id=device, device_id_type=MESH)

    data = images[...].astype(jnp.float32)
    for k in range(chunks):
        for c in range(chan):
            turn[pl.ds(k * ROWS + c, per, stride=chan), :] = data[
                c, :, k * LANES : (k + 1) * LANES
            ]
    lane = lax.broadcasted_iota(jnp.int32, (ROWS, LANES), 1)
    natural = [turn[k * ROWS : (k + 1) * ROWS, :] for k in range(chunks)]
    fold = LANES // SIDE
    for k in range(chunks):
        row = None
        for g in range(fold):
            at = g * chunks + k
            part = natural[at // fold]
            shift = (g - at % fold) * SIDE % LANES
            part = pltpu.roll(part, shift, 1) if shift else part
            row = part if row is None else jnp.where(lane >= g * SIDE, part, row)
        flat[pl.ds(k, per * chan, stride=chunks), :] = row[: per * chan]
    got[ROUNDS, z] = flat[...].astype(jnp.bfloat16)

    pl.semaphore_wait(barrier, len(partners))

    copies = []

    def give(order, source, d, device):
        copy = pltpu.make_async_remote_copy(
            src_ref=got.at[ROUNDS, source],
            dst_ref=got.at[ROUNDS - d, source],
            send_sem=send.at[order, ROUNDS + d],
            recv_sem=recv.at[ROUNDS - d, source],
            device_id=device,
            device_id_type=MESH,
        )
        copy.start()
        copies.append(copy)

    for order, d, device in sorted(partners, key=lambda p: p[0] < 2):
        give(order, z, d, device)

    masks = lane_masks()
    current = []
    for i in range(per):
        squares = []
        for k in range(chunks):
            parts = []
            for c in range(chan):
                row = i * image_rows + c * chunks + k
                part = jnp.broadcast_to(flat[row : row + 1, :], (ROWS, LANES))
                own[row] = part
                parts.append(part * part)
            squares.append(channel_sum(parts))
        current.append(squares)
    for layer in range(LAYERS):
        current = biased(stencil_sum(current, masks), map_scale(chan, layer))
        for i in range(per):
            roots, inverses = roots_of(current[i])
            for k in range(chunks):
                at = (i * LAYERS + layer) * chunks + k
                root[at] = roots[k]
                inv[at] = inverses[k]

    def arrived(k, source):
        pltpu.make_async_remote_copy(
            src_ref=got.at[k, source],
            dst_ref=got.at[k, source],
            send_sem=send.at[0, ROUNDS],
            recv_sem=recv.at[k, source],
            device_id={"grp": z},
            device_id_type=MESH,
        ).wait_recv()

    for order in range(2, n_grp):
        source = source_of(order)
        arrived(ROUNDS, source)
        for d in offsets:
            give(order, source, d, {"blk": lax.rem(b + d + n_blk, n_blk)})
    arrived(ROUNDS, source_of(1))

    def work(members):
        maps = []
        for m, (places, slot) in enumerate(members):
            for s, (k, source) in enumerate(places):
                wide[m, s * per * image_rows : (s + 1) * per * image_rows, :] = got[
                    k, source
                ].astype(jnp.float32)
            theirs = [
                [wide[m, pl.ds(c * chunks + j, ROWS, stride=image_rows), :] for c in range(chan)]
                for j in range(chunks)
            ]
            maps.append([channel_sum([x * x for x in parts]) for parts in theirs])
            for i in range(per):
                maps.append(
                    [
                        channel_sum(
                            [
                                own[i * image_rows + c * chunks + j] * theirs[j][c]
                                for c in range(chan)
                            ]
                        )
                        for j in range(chunks)
                    ]
                )
        for layer in range(LAYERS):
            maps = biased(stencil_sum(maps, masks), map_scale(chan, layer))
            for m in range(len(members)):
                roots, inverses = roots_of(maps[m * (per + 1)])
                for i in range(per):
                    at = (i * LAYERS + layer) * chunks
                    cov = maps[m * (per + 1) + 1 + i]
                    maps[m * (per + 1) + 1 + i] = [
                        twice_relu(cov[j], root[at + j] * roots[j], inv[at + j] * inverses[j])
                        for j in range(chunks)
                    ]
        for m, (places, slot) in enumerate(members):
            for i in range(per):
                res[i, slot] = channel_sum(maps[m * (per + 1) + 1 + i])

    def member(t):
        home = jnp.int32((t >= 1) & (t <= units))
        away = 1 - home
        order = jnp.where(t > units, t - units, 0)
        source = source_of(order)

        @pl.when(home == 0)
        def _():
            for d in offsets:
                arrived(ROUNDS + d, source)

        unit = home * (t - 1)
        places = [
            (ROUNDS + away * d, away * source + home * (unit * sources + s))
            for s, d in enumerate(offsets)
        ]
        return places, home * unit + away * (units + source)

    total_units = units + n_grp

    def step(t, carry):
        work([member(t)])
        return carry

    lax.fori_loop(0, total_units, step, 0)

    row = lax.broadcasted_iota(jnp.int32, (ROWS, LANES), 0)
    lane = lax.broadcasted_iota(jnp.int32, (ROWS, LANES), 1)
    for i in range(per):
        sums = [
            jnp.sum(res[i, slot], axis=1, keepdims=True)
            * (1.0 / (pix * map_scale(chan, LAYERS - 1)))
            for slot in range(units + n_grp)
        ]
        home = jnp.zeros((ROWS, LANES), jnp.float32)
        for unit in range(units):
            home = jnp.where(lane == row + unit * ROWS, sums[unit], home)
        out[ROUNDS, i : i + 1, :] = jnp.sum(home, axis=0, keepdims=True)[:, :block]
        away = jnp.zeros((ROWS, LANES), jnp.float32)
        for source in range(n_grp):
            mine = (lane // per == source) & (lane % per == row % per)
            away = jnp.where(mine, sums[units + source], away)
        total = away
        for r in range(1, per):
            total = total + pltpu.roll(away, ROWS - r, 0)
        for at, d in enumerate(offsets):
            out[ROUNDS + d, i : i + 1, :] = total[at * per : at * per + 1, :block]
    for copy in copies:
        copy.wait_send()


def per_device(n_blk, n_grp, images):
    per, chan, pix = images.shape
    chunks = pix // LANES
    rows = per * chan * chunks
    block = per * n_grp
    assert n_grp % 2 == 0 and block % ROWS == 0 and per * (SPAN - 1) == ROWS
    maps = per * LAYERS * chunks
    window = pl.pallas_call(
        functools.partial(kernel, n_blk, n_grp),
        out_shape=jax.ShapeDtypeStruct((SPAN, per, block), jnp.float32),
        in_specs=[pl.BlockSpec(memory_space=pltpu.VMEM)],
        out_specs=pl.BlockSpec(memory_space=pltpu.VMEM),
        scratch_shapes=[
            pltpu.VMEM((chunks * ROWS, LANES), jnp.float32),
            pltpu.VMEM((SPAN, n_grp, rows, LANES), jnp.bfloat16),
            pltpu.VMEM((rows, ROWS, LANES), jnp.float32),
            pltpu.VMEM((rows, LANES), jnp.float32),
            pltpu.VMEM((maps, ROWS, LANES), jnp.float32),
            pltpu.VMEM((maps, ROWS, LANES), jnp.float32),
            pltpu.VMEM((1, ROWS * chan * chunks, LANES), jnp.float32),
            pltpu.VMEM((per, block // ROWS + n_grp, ROWS, LANES), jnp.float32),
            pltpu.SemaphoreType.DMA((n_grp, SPAN)),
            pltpu.SemaphoreType.DMA((SPAN, n_grp)),
        ],
        compiler_params=pltpu.CompilerParams(
            collective_id=0, has_side_effects=True, vmem_limit_bytes=32 * 1024 * 1024
        ),
    )(jnp.transpose(images, (1, 0, 2)))
    return jnp.transpose(window, (1, 0, 2))


def solution(mesh):
    spec = P(("blk", "grp"), None, None)
    body = functools.partial(per_device, mesh.shape["blk"], mesh.shape["grp"])
    return jax.shard_map(body, mesh=mesh, in_specs=(spec,), out_specs=spec, check_vma=False)
```

```python
import functools

import jax
import jax.numpy as jnp
from jax import lax
from jax.experimental import pallas as pl
from jax.experimental.pallas import tpu as pltpu
from jax.sharding import PartitionSpec as P

SIDE = 32
LAYERS = 3
ROUNDS = 2
SPAN = 2 * ROUNDS + 1
LANES = 128
ROWS = 8
BIAS = 0.1
BELOW_ONE = 1.0 - 2.0**-24
MESH = pl.DeviceIdType.MESH

ARC = (
    0.3183095237082206,
    -0.02251588221055572,
    0.005816643278465437,
    -0.0019102241839555419,
    0.00040573672732109817,
)


def stencil_sum(groups, masks):
    first, last, not_left, not_right = masks
    tall = []
    for maps in groups:
        above = jnp.where(first, 0.0, pltpu.roll(maps[-1], SIDE, 1))
        below = jnp.where(last, 0.0, pltpu.roll(maps[0], LANES - SIDE, 1))
        column = [above] + list(maps) + [below]
        pairs = [x + y for x, y in zip(column[:-1], column[1:])]
        tall.append([pairs[k] + column[k + 2] for k in range(len(maps))])
    out = []
    for maps in tall:
        left = [jnp.where(not_left, pltpu.roll(x, 1, 1), 0.0) for x in maps]
        right = [jnp.where(not_right, pltpu.roll(x, LANES - 1, 1), 0.0) for x in maps]
        out.append([x + (y + z) for x, y, z in zip(maps, left, right)])
    return out


def lane_masks():
    lane = lax.broadcasted_iota(jnp.int32, (ROWS, LANES), 1)
    col = lane % SIDE
    return lane < SIDE, lane >= LANES - SIDE, col != 0, col != SIDE - 1


def channel_sum(terms):
    total = terms[0]
    for term in terms[1:]:
        total = total + term
    return total


def map_scale(channels, layer):
    return float(channels * 9 ** (layer + 1))


def biased(groups, scale):
    return [[x + BIAS * scale for x in maps] for maps in groups]


def roots_of(maps):
    inverse = [lax.rsqrt(x) for x in maps]
    return [x * y for x, y in zip(maps, inverse)], inverse


def twice_relu(cov, scale, inverse):
    a = jnp.minimum(jnp.abs(cov) * inverse, BELOW_ONE)
    y = 1.0 - a
    poly = ARC[-1]
    for c in ARC[-2::-1]:
        poly = poly * a + c
    bent = y * y * lax.rsqrt(y) * poly
    return scale * bent + jnp.minimum(jnp.maximum(cov, 0.0), scale)


def kernel(
    n_blk, n_grp, images, out, turn, got, own, flat, root, inv, wide, res,
    send, recv,
):
    b, z = lax.axis_index("blk"), lax.axis_index("grp")
    chan, per, pix = images.shape
    chunks = pix // LANES
    image_rows = chan * chunks
    block = per * n_grp
    units = block // ROWS
    sources = ROWS // per
    offsets = [d for d in range(-ROUNDS, ROUNDS + 1) if d]

    barrier = pltpu.get_barrier_semaphore()
    def source_of(order):
        if isinstance(order, int) and order == 0:
            return z
        mate = z + 1 - 2 * lax.rem(z, 2)
        far = lax.rem(z // 2 * 2 + order, n_grp)
        if isinstance(order, int):
            return mate if order == 1 else far
        return jnp.where(order == 0, z, jnp.where(order == 1, mate, far))

    partners = [(0, d) for d in offsets] + [(1, d) for d in [0] + offsets]
    partners += [(order, 0) for order in range(2, n_grp)]
    partners = [
        (order, d, {"blk": lax.rem(b + d + n_blk, n_blk), "grp": source_of(order)})
        for order, d in partners
    ]
    for order, d, device in partners:
        pl.semaphore_signal(barrier, inc=1, device_id=device, device_id_type=MESH)

    data = images[...].astype(jnp.float32)
    for k in range(chunks):
        for c in range(chan):
            turn[pl.ds(k * ROWS + c, per, stride=chan), :] = data[
                c, :, k * LANES : (k + 1) * LANES
            ]
    lane = lax.broadcasted_iota(jnp.int32, (ROWS, LANES), 1)
    natural = [turn[k * ROWS : (k + 1) * ROWS, :] for k in range(chunks)]
    fold = LANES // SIDE
    for k in range(chunks):
        row = None
        for g in range(fold):
            at = g * chunks + k
            part = natural[at // fold]
            shift = (g - at % fold) * SIDE % LANES
            part = pltpu.roll(part, shift, 1) if shift else part
            row = part if row is None else jnp.where(lane >= g * SIDE, part, row)
        flat[pl.ds(k, per * chan, stride=chunks), :] = row[: per * chan]
    got[ROUNDS, z] = flat[...].astype(jnp.bfloat16)

    pl.semaphore_wait(barrier, len(partners))

    copies = []

    def give(order, source, d, device):
        copy = pltpu.make_async_remote_copy(
            src_ref=got.at[ROUNDS, source],
            dst_ref=got.at[ROUNDS - d, source],
            send_sem=send.at[order, ROUNDS + d],
            recv_sem=recv.at[ROUNDS - d, source],
            device_id=device,
            device_id_type=MESH,
        )
        copy.start()
        copies.append(copy)

    for order, d, device in sorted(partners, key=lambda p: p[0] < 2):
        give(order, z, d, device)

    masks = lane_masks()
    current = []
    for i in range(per):
        squares = []
        for k in range(chunks):
            parts = []
            for c in range(chan):
                row = i * image_rows + c * chunks + k
                part = jnp.broadcast_to(flat[row : row + 1, :], (ROWS, LANES))
                own[row] = part
                parts.append(part * part)
            squares.append(channel_sum(parts))
        current.append(squares)
    for layer in range(LAYERS):
        current = biased(stencil_sum(current, masks), map_scale(chan, layer))
        for i in range(per):
            roots, inverses = roots_of(current[i])
            for k in range(chunks):
                at = (i * LAYERS + layer) * chunks + k
                root[at] = roots[k]
                inv[at] = inverses[k]

    def arrived(k, source):
        pltpu.make_async_remote_copy(
            src_ref=got.at[k, source],
            dst_ref=got.at[k, source],
            send_sem=send.at[0, ROUNDS],
            recv_sem=recv.at[k, source],
            device_id={"grp": z},
            device_id_type=MESH,
        ).wait_recv()

    for order in range(2, n_grp):
        source = source_of(order)
        arrived(ROUNDS, source)
        for d in offsets:
            give(order, source, d, {"blk": lax.rem(b + d + n_blk, n_blk)})
    arrived(ROUNDS, source_of(1))

    def work(members):
        maps = []
        for m, (places, slot) in enumerate(members):
            for s, (k, source) in enumerate(places):
                wide[m, s * per * image_rows : (s + 1) * per * image_rows, :] = got[
                    k, source
                ].astype(jnp.float32)
            theirs = [
                [wide[m, pl.ds(c * chunks + j, ROWS, stride=image_rows), :] for c in range(chan)]
                for j in range(chunks)
            ]
            maps.append([channel_sum([x * x for x in parts]) for parts in theirs])
            for i in range(per):
                maps.append(
                    [
                        channel_sum(
                            [
                                own[i * image_rows + c * chunks + j] * theirs[j][c]
                                for c in range(chan)
                            ]
                        )
                        for j in range(chunks)
                    ]
                )
        for layer in range(LAYERS):
            maps = biased(stencil_sum(maps, masks), map_scale(chan, layer))
            for m in range(len(members)):
                roots, inverses = roots_of(maps[m * (per + 1)])
                for i in range(per):
                    at = (i * LAYERS + layer) * chunks
                    cov = maps[m * (per + 1) + 1 + i]
                    maps[m * (per + 1) + 1 + i] = [
                        twice_relu(cov[j], root[at + j] * roots[j], inv[at + j] * inverses[j])
                        for j in range(chunks)
                    ]
        for m, (places, slot) in enumerate(members):
            for i in range(per):
                res[i, slot] = channel_sum(maps[m * (per + 1) + 1 + i])

    def member(t):
        home = jnp.int32((t >= 1) & (t <= units))
        away = 1 - home
        order = jnp.where(t > units, t - units, 0)
        source = source_of(order)

        @pl.when(home == 0)
        def _():
            for d in offsets:
                arrived(ROUNDS + d, source)

        unit = home * (t - 1)
        places = [
            (ROUNDS + away * d, away * source + home * (unit * sources + s))
            for s, d in enumerate(offsets)
        ]
        return places, home * unit + away * (units + source)

    total_units = units + n_grp

    def step(t, carry):
        work([member(t)])
        return carry

    lax.fori_loop(0, total_units, step, 0, unroll=True)

    row = lax.broadcasted_iota(jnp.int32, (ROWS, LANES), 0)
    lane = lax.broadcasted_iota(jnp.int32, (ROWS, LANES), 1)
    for i in range(per):
        sums = [
            jnp.sum(res[i, slot], axis=1, keepdims=True)
            * (1.0 / (pix * map_scale(chan, LAYERS - 1)))
            for slot in range(units + n_grp)
        ]
        home = jnp.zeros((ROWS, LANES), jnp.float32)
        for unit in range(units):
            home = jnp.where(lane == row + unit * ROWS, sums[unit], home)
        out[ROUNDS, i : i + 1, :] = jnp.sum(home, axis=0, keepdims=True)[:, :block]
        away = jnp.zeros((ROWS, LANES), jnp.float32)
        for source in range(n_grp):
            mine = (lane // per == source) & (lane % per == row % per)
            away = jnp.where(mine, sums[units + source], away)
        total = away
        for r in range(1, per):
            total = total + pltpu.roll(away, ROWS - r, 0)
        for at, d in enumerate(offsets):
            out[ROUNDS + d, i : i + 1, :] = total[at * per : at * per + 1, :block]
    for copy in copies:
        copy.wait_send()


def per_device(n_blk, n_grp, images):
    per, chan, pix = images.shape
    chunks = pix // LANES
    rows = per * chan * chunks
    block = per * n_grp
    assert n_grp % 2 == 0 and block % ROWS == 0 and per * (SPAN - 1) == ROWS
    maps = per * LAYERS * chunks
    window = pl.pallas_call(
        functools.partial(kernel, n_blk, n_grp),
        out_shape=jax.ShapeDtypeStruct((SPAN, per, block), jnp.float32),
        in_specs=[pl.BlockSpec(memory_space=pltpu.VMEM)],
        out_specs=pl.BlockSpec(memory_space=pltpu.VMEM),
        scratch_shapes=[
            pltpu.VMEM((chunks * ROWS, LANES), jnp.float32),
            pltpu.VMEM((SPAN, n_grp, rows, LANES), jnp.bfloat16),
            pltpu.VMEM((rows, ROWS, LANES), jnp.float32),
            pltpu.VMEM((rows, LANES), jnp.float32),
            pltpu.VMEM((maps, ROWS, LANES), jnp.float32),
            pltpu.VMEM((maps, ROWS, LANES), jnp.float32),
            pltpu.VMEM((1, ROWS * chan * chunks, LANES), jnp.float32),
            pltpu.VMEM((per, block // ROWS + n_grp, ROWS, LANES), jnp.float32),
            pltpu.SemaphoreType.DMA((n_grp, SPAN)),
            pltpu.SemaphoreType.DMA((SPAN, n_grp)),
        ],
        compiler_params=pltpu.CompilerParams(
            collective_id=0, has_side_effects=True, vmem_limit_bytes=32 * 1024 * 1024
        ),
    )(jnp.transpose(images, (1, 0, 2)))
    return jnp.transpose(window, (1, 0, 2))


def solution(mesh):
    spec = P(("blk", "grp"), None, None)
    body = functools.partial(per_device, mesh.shape["blk"], mesh.shape["grp"])
    return jax.shard_map(body, mesh=mesh, in_specs=(spec,), out_specs=spec, check_vma=False)
```

```python
import functools

import jax
import jax.numpy as jnp
from jax import lax
from jax.experimental import pallas as pl
from jax.experimental.pallas import tpu as pltpu
from jax.sharding import PartitionSpec as P

SIDE = 32
LAYERS = 3
ROUNDS = 2
SPAN = 2 * ROUNDS + 1
LANES = 128
ROWS = 8
BIAS = 0.1
BELOW_ONE = 1.0 - 2.0**-24
MESH = pl.DeviceIdType.MESH

ARC = (
    0.3183095237082206,
    -0.02251588221055572,
    0.005816643278465437,
    -0.0019102241839555419,
    0.00040573672732109817,
)


def stencil_sum(groups, masks):
    first, last, not_left, not_right = masks
    tall = []
    for maps in groups:
        above = jnp.where(first, 0.0, pltpu.roll(maps[-1], SIDE, 1))
        below = jnp.where(last, 0.0, pltpu.roll(maps[0], LANES - SIDE, 1))
        column = [above] + list(maps) + [below]
        pairs = [x + y for x, y in zip(column[:-1], column[1:])]
        tall.append([pairs[k] + column[k + 2] for k in range(len(maps))])
    out = []
    for maps in tall:
        left = [jnp.where(not_left, pltpu.roll(x, 1, 1), 0.0) for x in maps]
        right = [jnp.where(not_right, pltpu.roll(x, LANES - 1, 1), 0.0) for x in maps]
        out.append([x + (y + z) for x, y, z in zip(maps, left, right)])
    return out


def lane_masks():
    lane = lax.broadcasted_iota(jnp.int32, (ROWS, LANES), 1)
    col = lane % SIDE
    return lane < SIDE, lane >= LANES - SIDE, col != 0, col != SIDE - 1


def channel_sum(terms):
    total = terms[0]
    for term in terms[1:]:
        total = total + term
    return total


def map_scale(channels, layer):
    return float(channels * 9 ** (layer + 1))


def biased(groups, scale):
    return [[x + BIAS * scale for x in maps] for maps in groups]


def roots_of(maps):
    inverse = [lax.rsqrt(x) for x in maps]
    return [x * y for x, y in zip(maps, inverse)], inverse


def twice_relu(cov, scale, inverse):
    a = jnp.minimum(jnp.abs(cov) * inverse, BELOW_ONE)
    y = 1.0 - a
    poly = ARC[-1]
    for c in ARC[-2::-1]:
        poly = poly * a + c
    bent = y * y * lax.rsqrt(y) * poly
    return scale * bent + jnp.minimum(jnp.maximum(cov, 0.0), scale)


def kernel(
    n_blk, n_grp, images, out, turn, got, own, flat, root, inv, wide, res,
    send, recv,
):
    b, z = lax.axis_index("blk"), lax.axis_index("grp")
    chan, per, pix = images.shape
    chunks = pix // LANES
    image_rows = chan * chunks
    block = per * n_grp
    units = block // ROWS
    sources = ROWS // per
    offsets = [d for d in range(-ROUNDS, ROUNDS + 1) if d]

    barrier = pltpu.get_barrier_semaphore()
    def source_of(order):
        if isinstance(order, int) and order == 0:
            return z
        mate = z + 1 - 2 * lax.rem(z, 2)
        far = lax.rem(z // 2 * 2 + order, n_grp)
        if isinstance(order, int):
            return mate if order == 1 else far
        return jnp.where(order == 0, z, jnp.where(order == 1, mate, far))

    partners = [(0, d) for d in offsets] + [(1, d) for d in [0] + offsets]
    partners += [(order, 0) for order in range(2, n_grp)]
    partners = [
        (order, d, {"blk": lax.rem(b + d + n_blk, n_blk), "grp": source_of(order)})
        for order, d in partners
    ]
    for order, d, device in partners:
        pl.semaphore_signal(barrier, inc=1, device_id=device, device_id_type=MESH)

    data = images[...].astype(jnp.float32)
    for k in range(chunks):
        for c in range(chan):
            turn[pl.ds(k * ROWS + c, per, stride=chan), :] = data[
                c, :, k * LANES : (k + 1) * LANES
            ]
    lane = lax.broadcasted_iota(jnp.int32, (ROWS, LANES), 1)
    natural = [turn[k * ROWS : (k + 1) * ROWS, :] for k in range(chunks)]
    fold = LANES // SIDE
    for k in range(chunks):
        row = None
        for g in range(fold):
            at = g * chunks + k
            part = natural[at // fold]
            shift = (g - at % fold) * SIDE % LANES
            part = pltpu.roll(part, shift, 1) if shift else part
            row = part if row is None else jnp.where(lane >= g * SIDE, part, row)
        flat[pl.ds(k, per * chan, stride=chunks), :] = row[: per * chan]
    got[ROUNDS, z] = flat[...].astype(jnp.bfloat16)

    pl.semaphore_wait(barrier, len(partners))

    copies = []

    def give(order, source, d, device):
        copy = pltpu.make_async_remote_copy(
            src_ref=got.at[ROUNDS, source],
            dst_ref=got.at[ROUNDS - d, source],
            send_sem=send.at[order, ROUNDS + d],
            recv_sem=recv.at[ROUNDS - d, source],
            device_id=device,
            device_id_type=MESH,
        )
        copy.start()
        copies.append(copy)

    for order, d, device in sorted(partners, key=lambda p: p[0] < 2):
        give(order, z, d, device)

    masks = lane_masks()
    current = []
    for i in range(per):
        squares = []
        for k in range(chunks):
            parts = []
            for c in range(chan):
                row = i * image_rows + c * chunks + k
                part = jnp.broadcast_to(flat[row : row + 1, :], (ROWS, LANES))
                own[row] = part
                parts.append(part * part)
            squares.append(channel_sum(parts))
        current.append(squares)
    for layer in range(LAYERS):
        current = biased(stencil_sum(current, masks), map_scale(chan, layer))
        for i in range(per):
            roots, inverses = roots_of(current[i])
            for k in range(chunks):
                at = (i * LAYERS + layer) * chunks + k
                root[at] = roots[k]
                inv[at] = inverses[k]

    def arrived(k, source):
        pltpu.make_async_remote_copy(
            src_ref=got.at[k, source],
            dst_ref=got.at[k, source],
            send_sem=send.at[0, ROUNDS],
            recv_sem=recv.at[k, source],
            device_id={"grp": z},
            device_id_type=MESH,
        ).wait_recv()

    for order in range(2, n_grp):
        source = source_of(order)
        arrived(ROUNDS, source)
        for d in offsets:
            give(order, source, d, {"blk": lax.rem(b + d + n_blk, n_blk)})
    arrived(ROUNDS, source_of(1))

    def work(members):
        maps = []
        for m, (places, slot) in enumerate(members):
            for s, (k, source) in enumerate(places):
                wide[m, s * per * image_rows : (s + 1) * per * image_rows, :] = got[
                    k, source
                ].astype(jnp.float32)
            theirs = [
                [wide[m, pl.ds(c * chunks + j, ROWS, stride=image_rows), :] for c in range(chan)]
                for j in range(chunks)
            ]
            maps.append([channel_sum([x * x for x in parts]) for parts in theirs])
            for i in range(per):
                maps.append(
                    [
                        channel_sum(
                            [
                                own[i * image_rows + c * chunks + j] * theirs[j][c]
                                for c in range(chan)
                            ]
                        )
                        for j in range(chunks)
                    ]
                )
        for layer in range(LAYERS):
            maps = biased(stencil_sum(maps, masks), map_scale(chan, layer))
            for m in range(len(members)):
                roots, inverses = roots_of(maps[m * (per + 1)])
                for i in range(per):
                    at = (i * LAYERS + layer) * chunks
                    cov = maps[m * (per + 1) + 1 + i]
                    maps[m * (per + 1) + 1 + i] = [
                        twice_relu(cov[j], root[at + j] * roots[j], inv[at + j] * inverses[j])
                        for j in range(chunks)
                    ]
        for m, (places, slot) in enumerate(members):
            for i in range(per):
                res[i, slot] = channel_sum(maps[m * (per + 1) + 1 + i])

    def member(t):
        home = jnp.int32(t < units)
        away = 1 - home
        order = jnp.where(t > units, t - units, 0)
        source = source_of(order)

        @pl.when(home == 0)
        def _():
            for d in offsets:
                arrived(ROUNDS + d, source)

        unit = home * t
        places = [
            (ROUNDS + away * d, away * source + home * (unit * sources + s))
            for s, d in enumerate(offsets)
        ]
        return places, home * unit + away * (units + source)

    total_units = units + n_grp

    def step(t, carry):
        work([member(t)])
        return carry

    lax.fori_loop(0, total_units, step, 0, unroll=True)

    row = lax.broadcasted_iota(jnp.int32, (ROWS, LANES), 0)
    lane = lax.broadcasted_iota(jnp.int32, (ROWS, LANES), 1)
    for i in range(per):
        sums = [
            jnp.sum(res[i, slot], axis=1, keepdims=True)
            * (1.0 / (pix * map_scale(chan, LAYERS - 1)))
            for slot in range(units + n_grp)
        ]
        home = jnp.zeros((ROWS, LANES), jnp.float32)
        for unit in range(units):
            home = jnp.where(lane == row + unit * ROWS, sums[unit], home)
        out[ROUNDS, i : i + 1, :] = jnp.sum(home, axis=0, keepdims=True)[:, :block]
        away = jnp.zeros((ROWS, LANES), jnp.float32)
        for source in range(n_grp):
            mine = (lane // per == source) & (lane % per == row % per)
            away = jnp.where(mine, sums[units + source], away)
        total = away
        for r in range(1, per):
            total = total + pltpu.roll(away, ROWS - r, 0)
        for at, d in enumerate(offsets):
            out[ROUNDS + d, i : i + 1, :] = total[at * per : at * per + 1, :block]
    for copy in copies:
        copy.wait_send()


def per_device(n_blk, n_grp, images):
    per, chan, pix = images.shape
    chunks = pix // LANES
    rows = per * chan * chunks
    block = per * n_grp
    assert n_grp % 2 == 0 and block % ROWS == 0 and per * (SPAN - 1) == ROWS
    maps = per * LAYERS * chunks
    window = pl.pallas_call(
        functools.partial(kernel, n_blk, n_grp),
        out_shape=jax.ShapeDtypeStruct((SPAN, per, block), jnp.float32),
        in_specs=[pl.BlockSpec(memory_space=pltpu.VMEM)],
        out_specs=pl.BlockSpec(memory_space=pltpu.VMEM),
        scratch_shapes=[
            pltpu.VMEM((chunks * ROWS, LANES), jnp.float32),
            pltpu.VMEM((SPAN, n_grp, rows, LANES), jnp.bfloat16),
            pltpu.VMEM((rows, ROWS, LANES), jnp.float32),
            pltpu.VMEM((rows, LANES), jnp.float32),
            pltpu.VMEM((maps, ROWS, LANES), jnp.float32),
            pltpu.VMEM((maps, ROWS, LANES), jnp.float32),
            pltpu.VMEM((1, ROWS * chan * chunks, LANES), jnp.float32),
            pltpu.VMEM((per, block // ROWS + n_grp, ROWS, LANES), jnp.float32),
            pltpu.SemaphoreType.DMA((n_grp, SPAN)),
            pltpu.SemaphoreType.DMA((SPAN, n_grp)),
        ],
        compiler_params=pltpu.CompilerParams(
            collective_id=0, has_side_effects=True, vmem_limit_bytes=32 * 1024 * 1024
        ),
    )(jnp.transpose(images, (1, 0, 2)))
    return jnp.transpose(window, (1, 0, 2))


def solution(mesh):
    spec = P(("blk", "grp"), None, None)
    body = functools.partial(per_device, mesh.shape["blk"], mesh.shape["grp"])
    return jax.shard_map(body, mesh=mesh, in_specs=(spec,), out_specs=spec, check_vma=False)
```
